128 devices in a mesh: dp: 4 (over x_hi, core), ep: 32 (over x_lo, y, z).
Axes of the slice: x: 4 (x_hi: 2, x_lo: 2; x = x_hi * 2 + x_lo), y: 4, z: 4, core: 2. Of those that a mesh axis runs over, the one named last changes fastest.
Arguments:
- queries: bfloat16 [2048, 8192], P(('dp', 'ep')), may hold values from -40 to 40
- kv_cache: bfloat16 [2048, 2, 128, 512], P(('dp', 'ep')), may hold values from -40 to 40
- kv_new: bfloat16 [2048, 2, 512], P(('dp', 'ep')), may hold values from -40 to 40
- lengths: int32 [2048], P(('dp', 'ep')), may hold values from 1 to 128, as said below
- residual: bfloat16 [2048, 4096], P(('dp', 'ep')), may hold values from -64 to 64
- norm_gain: float32 [4096], replicated, may hold values from 0.1 to 1.9
- expert_ids: int32 [2048, 8], P(('dp', 'ep')), may hold values from 0 to 63, all different within a row; in each aligned block of 16 rows (0 to 15, 16 to 31, ...) at most 4 rows name the same one
- route_probs: float32 [2048, 8], P(('dp', 'ep')), may hold values from 0.05 to 1
- w_out: bfloat16 [8192, 4096], P(None, 'ep'), may hold values from -0.0625 to 0.0625
- w_gate: bfloat16 [64, 4096, 1536], P('ep', None, 'dp'), may hold values from -0.09375 to 0.09375
- w_up: bfloat16 [64, 4096, 1536], P('ep', None, 'dp'), may hold values from -0.09375 to 0.09375
- w_down: bfloat16 [64, 1536, 4096], P('ep', 'dp'), may hold values from -0.15625 to 0.15625
Outputs:
- attn_out: bfloat16 [2048, 4096], P(('dp', 'ep'))
- moe_out: bfloat16 [2048, 4096], P(('dp', 'ep'))
The draws below stay inside these ranges and needn't reach their ends.
Inputs may be any that keep to these rules, and one draw needn't show every extreme that they name: `lengths`: some row of the first device has all 128 positions valid. `expert_ids`: each row names 8 different experts; within the rows of one device no expert is named more than 4 times, a bound that some block reaches.
All inputs are finite; a program needn't handle non-finite values.
Results may differ from the reference program's by a relative error of at most 0.018.
Values may be sent and summed in bfloat16 or wider, within the bound.
No kernel may reach another device: no remote copies, remote signals or barrier semaphores. Data moves between devices by JAX's collectives and lax.ppermute only.
A program may use at most 128 MiB of HBM per device.

```python
import math
import jax
import jax.numpy as jnp
import numpy as np
from jax import lax

D = 4096
FF = 1536
HEADS = 64
KVH = 4
HD = 128
TOP = 8
SLOTS = 4
ROWS = 16
CAP = 128
EXPERTS = 64
TOKENS = 2048
N_DP = 4
N_EP = 32


def draw_queries(key, part):
    key = jax.random.fold_in(key, 11)
    values = jax.random.normal(key, (TOKENS, HEADS * HD), jnp.float32)
    return values.astype(jnp.bfloat16)


def draw_kv_cache(key, part):
    key = jax.random.fold_in(key, 21)
    values = jax.random.normal(key, (TOKENS, 2, CAP, KVH * HD), jnp.float32)
    return values.astype(jnp.bfloat16)


def draw_kv_new(key, part):
    key = jax.random.fold_in(key, 23)
    values = jax.random.normal(key, (TOKENS, 2, KVH * HD), jnp.float32)
    return values.astype(jnp.bfloat16)


def draw_lengths(key, part):
    key = jax.random.fold_in(key, 41)
    values = jax.random.randint(key, (TOKENS,), 1, CAP + 1, jnp.int32)
    return values.at[0].set(CAP)


def draw_residual(key, part):
    key = jax.random.fold_in(key, 31)
    first, second, third = jax.random.split(key, 3)
    values = jax.random.normal(first, (TOKENS, D), jnp.float32)
    row_scale = jnp.exp(jax.random.uniform(second, (TOKENS, 1), jnp.float32, math.log(0.3), math.log(3.0)))
    column_scale = jnp.exp(jax.random.uniform(third, (1, D), jnp.float32, math.log(0.3), math.log(3.0)))
    return jnp.clip(values * row_scale * column_scale, -60.0, 60.0).astype(jnp.bfloat16)


def shard_levels(rng, shape, cuts, low, top_value):
    loudness = 1.0
    for axis_at, blocks in cuts:
        steps = jax.random.uniform(jax.random.fold_in(jax.random.fold_in(rng, 6), axis_at), (blocks,), jnp.float32, low / len(cuts), top_value / len(cuts))
        loudness = loudness * jnp.repeat(jnp.exp(steps), shape[axis_at] // blocks).reshape((-1,) + (1,) * (len(shape) - 1 - axis_at))
    return loudness


def assign_block(own_key, own, number, rows, amount, top, most, lean):
    ranking = jax.random.permutation(own_key, amount)
    packed, usual = shares(amount, rows * top, most, lean, True), shares(amount, rows * top, most, lean, False)
    places = jnp.arange(amount)

    def named(sizes, rotation):
        used = int((sizes > 0).sum())
        fixed = max(1, used // 4)
        passed = fixed + (places - fixed + rotation * (used - fixed)) % max(1, amount - fixed)
        return jnp.zeros((amount,), jnp.int32).at[ranking[jnp.where(places < fixed, places, passed)]].set(jnp.asarray(sizes, jnp.int32))

    sizes = jnp.where(number % 4 == 0, named(packed, number // 4), named(usual, number - number // 4 - 1))
    mixed = jax.random.permutation(jax.random.fold_in(own, 3), amount)
    donor, receiver = mixed[0:amount // 2 * 2:2], mixed[1:amount // 2 * 2:2]
    margin = jnp.minimum(sizes[donor] - 1, most - sizes[receiver]) // 2
    margin = jnp.where((donor == ranking[0]) | (receiver == ranking[0]) | (sizes[receiver] == 0), 0, jnp.maximum(margin, 0))
    passed = jax.random.randint(jax.random.fold_in(own, 4), (amount // 2,), 0, 1 << 20) % (margin + 1)
    sizes = sizes.at[donor].add(-passed).at[receiver].add(passed)
    items = jnp.searchsorted(jnp.cumsum(sizes), jnp.arange(rows * top), side="right").astype(jnp.int32)
    table = items.reshape(top, rows).T
    table = table[jax.random.permutation(jax.random.fold_in(own, 1), rows)]
    rotation = jax.random.randint(jax.random.fold_in(own, 2), (rows, 1), 0, top)
    return jnp.take_along_axis(table, (jnp.arange(top)[None, :] + rotation) % top, axis=1)


def shares(count, total, limit, skew, full):
    portions = [(1 << 20) // math.isqrt(rank ** skew) + 1 for rank in range(1, count + 1)]
    largest = limit if full else min(limit, max(-(-total // count), total * portions[0] // sum(portions)))
    least = 1 if total - largest >= count - 1 else 0
    counts, surplus = [largest] + [least] * (count - 1), total - largest - least * (count - 1)
    while surplus > 0:
        free = [i for i in range(1, count) if counts[i] < largest] or [i for i in range(1, count) if counts[i] < limit]
        whole, remaining = sum([portions[i] for i in free]), surplus
        for i in free:
            extra = min(limit - counts[i], max(1, remaining * portions[i] // whole), surplus)
            counts[i] = counts[i] + extra
            surplus = surplus - extra
    return np.array(counts)


def centred(own_key, shape, spread, most, cuts=(), kind=jnp.bfloat16):
    entries = jax.random.normal(own_key, shape, jnp.float32) * spread
    if len(cuts) > 0:
        entries = shard_levels(own_key, shape, cuts, -0.22, 0.18) * entries
    return jnp.clip(entries, min=-most, max=most).astype(kind)


def setup_inputs(seed: int = 0) -> dict:
    key_list = jax.random.split(jax.random.key(seed), 13)
    queries = draw_queries(jax.random.fold_in(key_list[12], 71), 0)
    kv_cache = draw_kv_cache(jax.random.fold_in(key_list[12], 71), 0)
    kv_new = draw_kv_new(jax.random.fold_in(key_list[12], 71), 0)
    lengths = draw_lengths(jax.random.fold_in(key_list[12], 71), 0)
    residual = draw_residual(jax.random.fold_in(key_list[12], 71), 0)
    norm_gain = jnp.clip(1.0 + 0.18 * jax.random.normal(key_list[5], (D,), jnp.float32), 0.1, 1.9)
    expert_ids_keys = jax.random.split(jax.random.fold_in(key_list[6], 1), TOKENS // ROWS)
    expert_ids_turns = jax.random.permutation(jax.random.fold_in(key_list[6], 3), TOKENS // ROWS)
    expert_ids = jax.vmap(lambda own, number: assign_block(jax.random.fold_in(key_list[6], 2), own, number, ROWS, EXPERTS, TOP, SLOTS, 2))(expert_ids_keys, expert_ids_turns).reshape((TOKENS, TOP))
    route_probs = jnp.clip(jnp.exp(math.log(1.0) - 2.9957323 * jax.random.uniform(key_list[7], (TOKENS, TOP), jnp.float32) ** shard_levels(key_list[7], (TOKENS, TOP), ((0, 128),), -0.2, 0.2)), 0.05, 1.0)
    w_out = centred(key_list[8], (HEADS * HD, D), (HEADS * HD) ** -0.5, 0.0625, ((1, 32),))
    w_gate = centred(key_list[9], (EXPERTS, D, FF), D ** -0.5, 0.09375, ((0, 32), (2, 4)))
    w_up = centred(key_list[10], (EXPERTS, D, FF), D ** -0.5, 0.09375, ((0, 32), (2, 4)))
    w_down = centred(key_list[11], (EXPERTS, FF, D), FF ** -0.5, 0.15625, ((0, 32), (1, 4)))
    return dict(queries=queries, kv_cache=kv_cache, kv_new=kv_new, lengths=lengths, residual=residual, norm_gain=norm_gain, expert_ids=expert_ids, route_probs=route_probs, w_out=w_out, w_gate=w_gate, w_up=w_up, w_down=w_down)


def attend_block(inputs):
    query_block, cache_block, fresh_block, length_block = inputs
    block_rows = query_block.shape[0]
    groups = HEADS // KVH
    span_len = cache_block.shape[2]
    query_heads = query_block.astype(jnp.float32).reshape(block_rows, KVH, groups, HD)
    cache_keys = cache_block[:, 0].astype(jnp.float32).reshape(block_rows, span_len, KVH, HD)
    cache_values = cache_block[:, 1].astype(jnp.float32).reshape(block_rows, span_len, KVH, HD)
    fresh_keys = fresh_block[:, 0].astype(jnp.float32).reshape(block_rows, KVH, HD)
    fresh_values = fresh_block[:, 1].astype(jnp.float32).reshape(block_rows, KVH, HD)
    scaling = 1.0 / math.sqrt(HD)
    cache_scores = jnp.einsum('rkgd,rpkd->rkgp', query_heads, cache_keys, precision=lax.Precision.HIGHEST) * scaling
    live = jnp.arange(span_len, dtype=jnp.int32)[None, :] < length_block[:, None]
    cache_scores = jnp.where(live[:, None, None, :], cache_scores, -1e+30)
    fresh_scores = jnp.einsum('rkgd,rkd->rkg', query_heads, fresh_keys, precision=lax.Precision.HIGHEST) * scaling
    highest = jnp.maximum(lax.optimization_barrier(jnp.max(cache_scores, -1)), fresh_scores)
    cache_exp = jnp.exp(cache_scores - highest[..., None])
    fresh_exp = jnp.exp(fresh_scores - highest)
    denominator = lax.optimization_barrier(jnp.sum(cache_exp, -1)) + fresh_exp
    cache_weights = (cache_exp / denominator[..., None]).astype(jnp.bfloat16).astype(jnp.float32)
    fresh_weights = (fresh_exp / denominator).astype(jnp.bfloat16).astype(jnp.float32)
    mixed = jnp.einsum('rkgp,rpkd->rkgd', cache_weights, cache_values, precision=lax.Precision.HIGHEST)
    mixed = mixed + fresh_weights[..., None] * fresh_values[:, :, None, :]
    return mixed.reshape(block_rows, HEADS * HD).astype(jnp.bfloat16)

def reference(queries, kv_cache, kv_new, lengths, residual, norm_gain, expert_ids, route_probs, w_out, w_gate, w_up, w_down):
    token_count = queries.shape[0]
    block_count = token_count // 64
    attention = lax.map(attend_block, (queries.reshape(block_count, 64, HEADS * HD), kv_cache.reshape(block_count, 64, 2, CAP, KVH * HD), kv_new.reshape(block_count, 64, 2, KVH * HD), lengths.reshape(block_count, 64))).reshape(token_count, HEADS * HD)
    attn_out = jnp.dot(attention, w_out, preferred_element_type=jnp.float32).astype(jnp.bfloat16)
    stream = residual.astype(jnp.float32) + attn_out.astype(jnp.float32)
    normed = (stream * lax.rsqrt(lax.optimization_barrier(jnp.mean(stream * stream, -1, keepdims=True)) + 1e-06) * norm_gain).astype(jnp.bfloat16)
    gates = route_probs / lax.optimization_barrier(jnp.sum(route_probs, -1, keepdims=True))
    pair_ids = expert_ids.reshape(-1)
    pair_count = pair_ids.shape[0]
    most_rows = N_DP * N_EP * SLOTS
    share_width = FF // N_DP
    padded_rows = jnp.concatenate([normed, jnp.zeros((1, D), normed.dtype)], 0)

    def per_expert(totals, expert):
        chosen = jnp.nonzero(pair_ids == expert, size=most_rows, fill_value=pair_count)[0].astype(jnp.int32)
        source = jnp.where(chosen < pair_count, chosen // TOP, token_count).astype(jnp.int32)
        picked = padded_rows[source].astype(jnp.float32)
        gate_act = jnp.dot(picked, w_gate[expert].astype(jnp.float32), precision=lax.Precision.HIGHEST)
        up_act = jnp.dot(picked, w_up[expert].astype(jnp.float32), precision=lax.Precision.HIGHEST)
        hidden = (jax.nn.silu(gate_act) * up_act).astype(jnp.bfloat16)
        shard_terms = jnp.einsum('nsf,sfd->nsd', hidden.astype(jnp.float32).reshape(most_rows, N_DP, share_width), w_down[expert].astype(jnp.float32).reshape(N_DP, share_width, D), precision=lax.Precision.HIGHEST)
        rounded = lax.optimization_barrier(shard_terms.astype(jnp.bfloat16)).astype(jnp.float32)
        return (totals.at[chosen].add(lax.optimization_barrier(jnp.sum(rounded, 1))), None)
    starting = jnp.zeros((pair_count + 1, D), jnp.float32)
    totals = lax.scan(per_expert, starting, jnp.arange(EXPERTS, dtype=jnp.int32))[0]
    summed = lax.optimization_barrier(totals[:pair_count].astype(jnp.bfloat16)).astype(jnp.float32)
    expert_out = summed.reshape(token_count, TOP, D)
    moe_out = lax.optimization_barrier(jnp.sum(gates[:, :, None] * expert_out, 1)).astype(jnp.bfloat16)
    return (attn_out, moe_out)
```

```python
import math

import jax
import jax.numpy as jnp
from jax import lax
from jax.experimental import pallas as pl
from jax.experimental.pallas import tpu as pltpu
from jax.sharding import Mesh, PartitionSpec as P

HEADS = 64
KVH = 4
HD = 128
TOP = 8
SLOTS = 4

DP = ("xh", "core")
EP = ("xl", "yh", "yl", "z")
SPLIT = ("yl", "z")
CHIPS = ("xh",) + EP
ALL = DP + EP
SWAP = ((0, 1), (1, 0))
MIB = 1 << 20


def attend(queries, kv_cache, kv_new, lengths):
    row_count = queries.shape[0]
    groups = HEADS // KVH
    span_len = kv_cache.shape[2]
    query_heads = queries.reshape(row_count, KVH, groups, HD)
    cache_keys = kv_cache[:, 0].reshape(row_count, span_len, KVH, HD)
    cache_values = kv_cache[:, 1].reshape(row_count, span_len, KVH, HD)
    fresh_keys = kv_new[:, 0].reshape(row_count, KVH, HD)
    fresh_values = kv_new[:, 1].reshape(row_count, KVH, HD)
    scaling = 1.0 / math.sqrt(HD)
    cache_scores = (
        jnp.einsum("rkgd,rpkd->rkgp", query_heads, cache_keys, preferred_element_type=jnp.float32)
        * scaling
    )
    live = jnp.arange(span_len, dtype=jnp.int32)[None, :] < lengths[:, None]
    cache_scores = jnp.where(live[:, None, None, :], cache_scores, -1e30)
    fresh_scores = (
        jnp.einsum("rkgd,rkd->rkg", query_heads, fresh_keys, preferred_element_type=jnp.float32)
        * scaling
    )
    highest = jnp.maximum(jnp.max(cache_scores, -1), fresh_scores)
    cache_exp = jnp.exp(cache_scores - highest[..., None])
    fresh_exp = jnp.exp(fresh_scores - highest)
    denominator = jnp.sum(cache_exp, -1) + fresh_exp
    cache_weights = (cache_exp / denominator[..., None]).astype(jnp.bfloat16)
    fresh_weights = (fresh_exp / denominator).astype(jnp.bfloat16)
    mixed = jnp.einsum(
        "rkgp,rpkd->rkgd", cache_weights, cache_values, preferred_element_type=jnp.float32
    )
    mixed = mixed + jnp.einsum(
        "rkg,rkd->rkgd", fresh_weights, fresh_values, preferred_element_type=jnp.float32
    )
    return mixed.reshape(row_count, HEADS * HD).astype(jnp.bfloat16)


def expert_kernel(
    core_ref,
    rows_hbm,
    gate_a,
    up_a,
    down_a,
    gate_b,
    up_b,
    down_b,
    out_ref,
    rows,
    gate,
    up,
    down,
    hidden,
    sems,
):
    mine = core_ref[0]
    copies = [pltpu.make_async_copy(rows_hbm, rows, sems.at[0])]
    sources = ((gate_a, gate, 0), (up_a, up, 0), (gate_b, gate, 1), (up_b, up, 1), (down_a, down, 0), (down_b, down, 1))
    for number, (source, target, place) in enumerate(sources):
        copies.append(pltpu.make_async_copy(source.at[mine], target.at[place], sems.at[number + 1]))
    for copy in copies:
        copy.start()
    copies[0].wait()
    share = gate.shape[2]
    step = 128
    for place in range(2):
        copies[1 + 2 * place].wait()
        copies[2 + 2 * place].wait()

        @pl.loop(0, share // step)
        def _(block, place=place):
            columns = pl.ds(pl.multiple_of(block * step, step), step)
            both = jnp.concatenate([gate[place, :, columns], up[place, :, columns]], axis=1)
            acts = jnp.dot(rows[...], both, preferred_element_type=jnp.float32)
            gate_act = acts[:, :step]
            value = gate_act / (1.0 + jnp.exp(-gate_act)) * acts[:, step:]
            at = pl.ds(pl.multiple_of(place * share + block * step, step), step)
            hidden[:, at] = value.astype(jnp.bfloat16)

    copies[5].wait()
    copies[6].wait()
    width = 512

    @pl.loop(0, out_ref.shape[1] // width)
    def _(block):
        columns = pl.ds(pl.multiple_of(block * width, width), width)
        both = jnp.concatenate([down[0, :, columns], down[1, :, columns]], axis=0)
        out_ref[:, columns] = jnp.dot(
            hidden[...], both, preferred_element_type=jnp.float32
        ).astype(out_ref.dtype)


def run_expert(core, rows, gate_a, up_a, down_a, gate_b, up_b, down_b):
    count, depth = rows.shape
    share = gate_a.shape[2]
    hbm = pl.BlockSpec(memory_space=pl.ANY)
    return pl.pallas_call(
        expert_kernel,
        out_shape=jax.ShapeDtypeStruct((count, depth), jnp.bfloat16),
        in_specs=[pl.BlockSpec(memory_space=pltpu.SMEM)] + [hbm] * 7,
        out_specs=pl.BlockSpec(memory_space=pltpu.VMEM),
        scratch_shapes=[
            pltpu.VMEM((count, depth), jnp.bfloat16),
            pltpu.VMEM((2, depth, share), jnp.bfloat16),
            pltpu.VMEM((2, depth, share), jnp.bfloat16),
            pltpu.VMEM((2, share, depth), jnp.bfloat16),
            pltpu.VMEM((count, 2 * share), jnp.bfloat16),
            pltpu.SemaphoreType.DMA((7,)),
        ],
        compiler_params=pltpu.CompilerParams(vmem_limit_bytes=56 * MIB),
        cost_estimate=pl.CostEstimate(
            flops=2 * count * depth * share * 6,
            bytes_accessed=2 * (2 * count * depth + 6 * depth * share),
            transcendentals=count * share * 2,
        ),
    )(core, rows, gate_a, up_a, down_a, gate_b, up_b, down_b)


def swap(value):
    return lax.ppermute(value, "core", SWAP)


def places(expert_ids, core, expert_total):
    row_count = expert_ids.shape[0]
    pair_ids = expert_ids.reshape(-1)
    member = (pair_ids[:, None] == jnp.arange(expert_total, dtype=jnp.int32)[None, :]).astype(
        jnp.int32
    )
    ranking = jnp.sum((jnp.cumsum(member, 0) - 1) * member, 1)
    here = (pair_ids % 2) == core
    slot = (pair_ids // 2) * (2 * SLOTS) + ranking
    slot = jnp.where(here, slot, -1)
    return slot.reshape(row_count, TOP)


def on_device(
    queries,
    kv_cache,
    kv_new,
    lengths,
    residual,
    norm_gain,
    expert_ids,
    route_probs,
    w_out,
    w_gate,
    w_up,
    w_down,
):
    row_count = queries.shape[0]
    core = lax.axis_index("core")
    ep_size = lax.axis_size(EP)
    parts = lax.axis_size(SPLIT)
    groups = ep_size // parts
    chips = lax.axis_size(CHIPS)
    depth = w_out.shape[0] // parts
    half = depth // 2
    width = w_out.shape[1]

    mine = lax.dynamic_index_in_dim(
        w_out.reshape(parts, 2, half, width), core, axis=1, keepdims=False
    )
    mine = lax.all_to_all(mine, SPLIT, split_axis=0, concat_axis=0, tiled=True)
    other = swap(mine)
    low = jnp.where(core == 0, mine, other)
    high = jnp.where(core == 0, other, mine)
    weights = jnp.stack([low, high], 1).reshape(parts, depth, width)
    weights = weights.transpose(1, 0, 2).reshape(depth, parts * width)

    gate_b, up_b, down_b = swap(w_gate), swap(w_up), swap(w_down)

    expert_total = w_gate.shape[0] * ep_size
    slot_total = 2 * SLOTS * ep_size
    gates = route_probs / jnp.sum(route_probs, -1, keepdims=True)
    own_slots = places(expert_ids, core, expert_total)
    other_slots = places(swap(expert_ids), core, expert_total)
    other_slots = jnp.where(other_slots >= 0, other_slots + SLOTS, -1)
    slots = jnp.concatenate([own_slots, other_slots], 0)
    both_gates = jnp.concatenate([gates, swap(gates)], 0)
    chosen = slots[:, :, None] == jnp.arange(slot_total, dtype=jnp.int32)[None, None, :]
    placing = jnp.any(chosen, 1)
    mixing = jnp.sum(jnp.where(chosen, both_gates[:, :, None], 0.0), 1)
    placing = jnp.concatenate([placing, placing], 1).astype(jnp.bfloat16)
    mixing = jnp.concatenate([mixing, mixing], 1)
    mixing_high = mixing.astype(jnp.bfloat16)
    mixing_low = (mixing - mixing_high.astype(jnp.float32)).astype(jnp.bfloat16)
    mixing = jnp.concatenate([mixing_high, mixing_low], 0)

    attention = attend(queries, kv_cache, kv_new, lengths)
    sent = attention.reshape(row_count, parts, depth).transpose(1, 0, 2)
    sent = jnp.broadcast_to(sent[None], (groups, parts, row_count, depth))
    sent = sent.reshape(ep_size, row_count, depth)
    gathered = lax.all_to_all(sent, EP, split_axis=0, concat_axis=0, tiled=True)
    columns = jnp.dot(
        gathered.reshape(ep_size * row_count, depth), weights, preferred_element_type=jnp.float32
    ).astype(jnp.bfloat16)
    terms = lax.all_to_all(
        columns.reshape(ep_size, row_count, parts * width), EP, split_axis=0, concat_axis=0, tiled=True
    )
    terms = terms.reshape(groups, parts, row_count, parts * width)
    summed = jnp.sum(terms.astype(jnp.float32), 1).astype(jnp.bfloat16)
    attn_out = summed.transpose(1, 0, 2).reshape(row_count, ep_size * width)
    stream = residual.astype(jnp.float32) + attn_out.astype(jnp.float32)
    normed = (
        stream * lax.rsqrt(jnp.mean(stream * stream, -1, keepdims=True) + 1e-06) * norm_gain
    ).astype(jnp.bfloat16)

    rows = jnp.concatenate([normed, swap(normed)], 0)
    outgoing = lax.dot_general(
        placing, rows, (((0,), (0,)), ((), ())), preferred_element_type=jnp.float32
    ).astype(jnp.bfloat16)
    arrived = lax.all_to_all(
        outgoing.reshape(chips, 2 * SLOTS, -1), CHIPS, split_axis=0, concat_axis=0, tiled=True
    )
    partial_value = run_expert(
        core.astype(jnp.int32).reshape(1),
        arrived.reshape(chips * 2 * SLOTS, -1),
        w_gate,
        w_up,
        w_down,
        gate_b,
        up_b,
        down_b,
    )
    returned = lax.all_to_all(
        partial_value.reshape(chips, 2 * SLOTS, -1), CHIPS, split_axis=0, concat_axis=0, tiled=True
    )
    mixed = jnp.dot(
        mixing, returned.reshape(chips * 2 * SLOTS, -1), preferred_element_type=jnp.float32
    )
    mixed = mixed[: 2 * row_count] + mixed[2 * row_count :]
    moe_out = mixed[:row_count] + swap(mixed[row_count:])
    return (attn_out, moe_out.astype(jnp.bfloat16))


def solution(mesh):
    fine = Mesh(mesh.devices.reshape(2, 2, 2, 2, 2, 4), ALL)
    return jax.shard_map(
        on_device,
        mesh=fine,
        in_specs=(
            P(ALL, None),
            P(ALL, None, None, None),
            P(ALL, None, None),
            P(ALL),
            P(ALL, None),
            P(),
            P(ALL, None),
            P(ALL, None),
            P(None, EP),
            P(EP, None, DP),
            P(EP, None, DP),
            P(EP, DP, None),
        ),
        out_specs=(P(ALL, None), P(ALL, None)),
        check_vma=False,
    )
```

```python
import functools
import math

import jax
import jax.numpy as jnp
from jax import lax
from jax.experimental import pallas as pl
from jax.experimental.pallas import tpu as pltpu
from jax.sharding import Mesh, PartitionSpec as P

HEADS = 64
KVH = 4
HD = 128
TOP = 8
SLOTS = 4

DP = ("xh", "core")
EP = ("xl", "yh", "yl", "z")
SPLIT = ("yl", "z")
CHIPS = ("xh",) + EP
ALL = DP + EP
SWAP = ((0, 1), (1, 0))
MIB = 1 << 20
BLOCK = 128
WIDE = 512
PIECE = 1024
AHEAD = 8


def attend_kernel(lengths_ref, queries_ref, cache_hbm, fresh_ref, out_ref, cache, heads, sems, *, parts, copies):
    rows = queries_ref.shape[0]
    batch = rows // sems.shape[0]
    span = cache.shape[2]
    moves = []
    for number in range(sems.shape[0]):
        at = pl.ds(number * batch, batch)
        moves.append(pltpu.make_async_copy(cache_hbm.at[at], cache.at[at], sems.at[number]))
        moves[-1].start()
    groups = HEADS // KVH
    scaling = 1.0 / math.sqrt(HD)
    for head in range(HEADS):
        heads[pl.ds(head, rows, stride=HEADS), :] = queries_ref[:, head * HD : (head + 1) * HD].astype(jnp.float32)
    position = lax.broadcasted_iota(jnp.int32, (HEADS, span), 1)
    for row in range(rows):
        if row % batch == 0:
            moves[row // batch].wait()
        at = slice(row * HEADS, (row + 1) * HEADS)
        query = heads[at, :]
        query16 = query.astype(jnp.bfloat16)
        scores = []
        fresh = []
        for k in range(KVH):
            cols = slice(k * HD, (k + 1) * HD)
            own = slice(k * groups, (k + 1) * groups)
            scores.append(
                lax.dot_general(
                    query16[own], cache[row, 0, :, cols], (((1,), (1,)), ((), ())), preferred_element_type=jnp.float32
                )
            )
            key = fresh_ref[row, 0:1, cols].astype(jnp.float32)
            fresh.append(jnp.sum(query[own] * key, axis=1, keepdims=True))
        scores = jnp.concatenate(scores, 0) * scaling
        fresh = jnp.concatenate(fresh, 0) * scaling
        scores = jnp.where(position < lengths_ref[row], scores, -1e30)
        highest = jnp.maximum(jnp.max(scores, axis=1, keepdims=True), fresh)
        scores = jnp.exp(scores - highest)
        fresh = jnp.exp(fresh - highest)
        denominator = jnp.sum(scores, axis=1, keepdims=True) + fresh
        weights = (scores / denominator).astype(jnp.bfloat16)
        fresh = (fresh / denominator).astype(jnp.bfloat16).astype(jnp.float32)
        mixed = []
        for k in range(KVH):
            cols = slice(k * HD, (k + 1) * HD)
            own = slice(k * groups, (k + 1) * groups)
            value = jnp.dot(weights[own], cache[row, 1, :, cols], preferred_element_type=jnp.float32)
            mixed.append(value + fresh[own] * fresh_ref[row, 1:2, cols].astype(jnp.float32))
        heads[at, :] = jnp.concatenate(mixed, 0)
    share = HEADS // parts
    for head in range(HEADS):
        value = heads[pl.ds(head, rows, stride=HEADS), :].astype(jnp.bfloat16)
        cols = slice(head % share * HD, (head % share + 1) * HD)
        for copy in range(copies):
            out_ref[copy * parts + head // share, :, cols] = value

def run_attend(queries, kv_cache, kv_new, lengths, parts, copies):
    rows = queries.shape[0]
    return pl.pallas_call(
        functools.partial(attend_kernel, parts=parts, copies=copies),
        out_shape=jax.ShapeDtypeStruct((copies * parts, rows, HEADS * HD // parts), jnp.bfloat16),
        in_specs=[pl.BlockSpec(memory_space=pltpu.SMEM), pl.BlockSpec(memory_space=pltpu.VMEM), pl.BlockSpec(memory_space=pl.ANY), pl.BlockSpec(memory_space=pltpu.VMEM)],
        out_specs=pl.BlockSpec(memory_space=pltpu.VMEM),
        scratch_shapes=[pltpu.VMEM(kv_cache.shape, jnp.bfloat16), pltpu.VMEM((rows * HEADS, HD), jnp.float32), pltpu.SemaphoreType.DMA((4,))],
        compiler_params=pltpu.CompilerParams(vmem_limit_bytes=24 * MIB),
        cost_estimate=pl.CostEstimate(
            flops=4 * kv_cache.size // 2 * HEADS // KVH,
            bytes_accessed=2 * (kv_cache.size + 5 * queries.size),
            transcendentals=rows * HEADS * kv_cache.shape[2],
        ),
        name="attend",
    )(lengths, queries, kv_cache, kv_new)


def expert_kernel(
    core_ref, rows_hbm, gate_a, up_a, down_a, gate_b, up_b, down_b, out_hbm, rows, gate, up, down, hidden, out, sems, out_sems
):
    mine = core_ref[0]
    depth = rows.shape[1]
    share = gate.shape[2]
    blocks = share // BLOCK
    pieces = depth // PIECE
    moves = []

    def move(source, target):
        moves.append(pltpu.make_async_copy(source, target, sems.at[len(moves)]))
        return len(moves) - 1

    def at(block):
        return pl.ds(block * BLOCK, BLOCK)

    in_gate = ((gate_a, gate.at[0]), (gate_b, gate.at[1]))
    in_up = ((up_a, up.at[0]), (up_b, up.at[1]))
    in_down = ((down_a, down.at[0]), (down_b, down.at[1]))
    first = []
    for piece in range(pieces):
        part = pl.ds(piece * PIECE, PIECE)
        for source, target in (in_gate[0], in_up[0]):
            last = move(source.at[mine, part, at(0)], target.at[part, at(0)])
        last = move(rows_hbm.at[:, part], rows.at[:, part])
        first.append(last)
    later = {}
    for place in range(2):
        for block in range(blocks):
            if place + block > 0:
                for source, target in (in_gate[place], in_up[place]):
                    later[place, block] = move(source.at[mine, :, at(block)], target.at[:, at(block)])
    finals = []
    for block in range(depth // WIDE):
        part = pl.ds(block * WIDE, WIDE)
        for source, target in in_down:
            last = move(source.at[mine, :, part], target.at[:, part])
        finals.append(last)

    state = {"started": 0, "waited": 0}

    def reach(number):
        while state["started"] < min(len(moves), number + 1 + AHEAD):
            moves[state["started"]].start()
            state["started"] += 1
        while state["waited"] <= number:
            moves[state["waited"]].wait()
            state["waited"] += 1

    for place in range(2):
        for block in range(blocks):
            cols = slice(block * BLOCK, (block + 1) * BLOCK)
            if place + block == 0:
                acts = None
                for piece in range(pieces):
                    reach(first[piece])
                    part = slice(piece * PIECE, (piece + 1) * PIECE)
                    both = jnp.concatenate([gate[place, part, cols], up[place, part, cols]], axis=1)
                    term = jnp.dot(rows[:, part], both, preferred_element_type=jnp.float32)
                    acts = term if acts is None else acts + term
            else:
                reach(later[place, block])
                both = jnp.concatenate([gate[place, :, cols], up[place, :, cols]], axis=1)
                acts = jnp.dot(rows[...], both, preferred_element_type=jnp.float32)
            gate_act = acts[:, :BLOCK]
            value = gate_act / (1.0 + jnp.exp(-gate_act)) * acts[:, BLOCK:]
            start = place * share + block * BLOCK
            hidden[:, start : start + BLOCK] = value.astype(jnp.bfloat16)

    stores = []
    for block in range(depth // WIDE):
        reach(finals[block])
        cols = slice(block * WIDE, (block + 1) * WIDE)
        both = jnp.concatenate([down[0, :, cols], down[1, :, cols]], axis=0)
        out[:, cols] = jnp.dot(hidden[...], both, preferred_element_type=jnp.float32).astype(out.dtype)
        part = pl.ds(block * WIDE, WIDE)
        stores.append(pltpu.make_async_copy(out.at[:, part], out_hbm.at[:, part], out_sems.at[block]))
        stores[-1].start()
    for store in stores:
        store.wait()


def run_expert(core, rows, gate_a, up_a, down_a, gate_b, up_b, down_b):
    count, depth = rows.shape
    share = gate_a.shape[2]
    moves = 3 * (depth // PIECE) + 2 * (2 * share // BLOCK - 1) + 2 * (depth // WIDE)
    hbm = pl.BlockSpec(memory_space=pl.ANY)
    return pl.pallas_call(
        expert_kernel,
        out_shape=jax.ShapeDtypeStruct((count, depth), jnp.bfloat16),
        in_specs=[pl.BlockSpec(memory_space=pltpu.SMEM)] + [hbm] * 7,
        out_specs=hbm,
        scratch_shapes=[
            pltpu.VMEM((count, depth), jnp.bfloat16),
            pltpu.VMEM((2, depth, share), jnp.bfloat16),
            pltpu.VMEM((2, depth, share), jnp.bfloat16),
            pltpu.VMEM((2, share, depth), jnp.bfloat16),
            pltpu.VMEM((count, 2 * share), jnp.bfloat16),
            pltpu.VMEM((count, depth), jnp.bfloat16),
            pltpu.SemaphoreType.DMA((moves,)),
            pltpu.SemaphoreType.DMA((depth // WIDE,)),
        ],
        compiler_params=pltpu.CompilerParams(vmem_limit_bytes=48 * MIB),
        cost_estimate=pl.CostEstimate(
            flops=2 * count * depth * share * 6,
            bytes_accessed=2 * (2 * count * depth + 6 * depth * share),
            transcendentals=count * share * 2,
        ),
        name="expert",
    )(core, rows, gate_a, up_a, down_a, gate_b, up_b, down_b)


def project_kernel(core_ref, rows_ref, mine_ref, other_ref, out_ref):
    mine = core_ref[0]
    half = mine_ref.shape[1]
    width = mine_ref.shape[2]
    near = rows_ref[:, pl.ds(pl.multiple_of(mine * half, half), half)]
    far = rows_ref[:, pl.ds(pl.multiple_of((1 - mine) * half, half), half)]
    for block in range(0, mine_ref.shape[0], 2):
        weights = jnp.concatenate([mine_ref[block], mine_ref[block + 1]], axis=1)
        total = jnp.dot(near, weights, preferred_element_type=jnp.float32)
        weights = jnp.concatenate([other_ref[block], other_ref[block + 1]], axis=1)
        total += jnp.dot(far, weights, preferred_element_type=jnp.float32)
        out_ref[:, block * width : (block + 2) * width] = total.astype(out_ref.dtype)


def run_project(core, rows, mine, other):
    count, depth = rows.shape
    width = mine.shape[0] * mine.shape[2]
    vmem = pl.BlockSpec(memory_space=pltpu.VMEM)
    return pl.pallas_call(
        project_kernel,
        out_shape=jax.ShapeDtypeStruct((count, width), jnp.bfloat16),
        in_specs=[pl.BlockSpec(memory_space=pltpu.SMEM)] + [vmem] * 3,
        out_specs=vmem,
        compiler_params=pltpu.CompilerParams(vmem_limit_bytes=16 * MIB),
        cost_estimate=pl.CostEstimate(
            flops=2 * count * depth * width,
            bytes_accessed=2 * (count * depth + count * width + depth * width),
            transcendentals=0,
        ),
        name="project",
    )(core, rows, mine, other)


def norm_kernel(terms_ref, residual_ref, gain_ref, out_ref, normed_ref, *, parts):
    width = terms_ref.shape[2]
    streams = []
    squares = None
    for group in range(terms_ref.shape[0] // parts):
        cols = slice(group * width, (group + 1) * width)
        total = terms_ref[group * parts].astype(jnp.float32)
        for part in range(1, parts):
            total += terms_ref[group * parts + part].astype(jnp.float32)
        total = total.astype(jnp.bfloat16)
        out_ref[:, cols] = total
        stream = residual_ref[:, cols].astype(jnp.float32) + total.astype(jnp.float32)
        square = jnp.sum(stream * stream, axis=1, keepdims=True)
        squares = square if squares is None else squares + square
        streams.append(stream)
    scale = lax.rsqrt(squares / out_ref.shape[1] + 1e-06)
    for group, stream in enumerate(streams):
        cols = slice(group * width, (group + 1) * width)
        normed_ref[:, cols] = (stream * scale * gain_ref[:, cols]).astype(jnp.bfloat16)


def run_norm(terms, residual, gain, parts):
    vmem = pl.BlockSpec(memory_space=pltpu.VMEM)
    return pl.pallas_call(
        functools.partial(norm_kernel, parts=parts),
        out_shape=[jax.ShapeDtypeStruct(residual.shape, jnp.bfloat16)] * 2,
        in_specs=[vmem] * 3,
        out_specs=[vmem] * 2,
        compiler_params=pltpu.CompilerParams(vmem_limit_bytes=16 * MIB),
        cost_estimate=pl.CostEstimate(
            flops=2 * terms.size, bytes_accessed=2 * terms.size, transcendentals=0
        ),
        name="norm",
    )(terms, residual, gain.reshape(1, -1))


def swap(value):
    return lax.ppermute(value, "core", SWAP)


def places(expert_ids, core, expert_total):
    row_count = expert_ids.shape[0]
    pair_ids = expert_ids.reshape(-1)
    member = (pair_ids[:, None] == jnp.arange(expert_total, dtype=jnp.int32)[None, :]).astype(
        jnp.int32
    )
    ranking = jnp.sum((jnp.cumsum(member, 0) - 1) * member, 1)
    here = (pair_ids % 2) == core
    slot = (pair_ids // 2) * (2 * SLOTS) + ranking
    slot = jnp.where(here, slot, -1)
    return slot.reshape(row_count, TOP)


def on_device(
    queries,
    kv_cache,
    kv_new,
    lengths,
    residual,
    norm_gain,
    expert_ids,
    route_probs,
    w_out,
    w_gate,
    w_up,
    w_down,
):
    row_count = queries.shape[0]
    core = lax.axis_index("core")
    core_index = core.astype(jnp.int32).reshape(1)
    ep_size = lax.axis_size(EP)
    parts = lax.axis_size(SPLIT)
    groups = ep_size // parts
    chips = lax.axis_size(CHIPS)
    depth = w_out.shape[0] // parts
    half = depth // 2
    width = w_out.shape[1]

    mine = lax.dynamic_index_in_dim(
        w_out.reshape(parts, 2, half, width), core, axis=1, keepdims=False
    )
    mine = lax.all_to_all(mine, SPLIT, split_axis=0, concat_axis=0, tiled=True)
    other = swap(mine)

    gate_b, up_b, down_b = swap(w_gate), swap(w_up), swap(w_down)

    expert_total = w_gate.shape[0] * ep_size
    slot_total = 2 * SLOTS * ep_size
    gates = route_probs / jnp.sum(route_probs, -1, keepdims=True)
    own_slots = places(expert_ids, core, expert_total)
    other_slots = places(swap(expert_ids), core, expert_total)
    other_slots = jnp.where(other_slots >= 0, other_slots + SLOTS, -1)
    slots = jnp.concatenate([own_slots, other_slots], 0)
    both_gates = jnp.concatenate([gates, swap(gates)], 0)
    chosen = slots[:, :, None] == jnp.arange(slot_total, dtype=jnp.int32)[None, None, :]
    placing = jnp.any(chosen, 1)
    mixing = jnp.sum(jnp.where(chosen, both_gates[:, :, None], 0.0), 1)
    placing = jnp.concatenate([placing, placing], 1).astype(jnp.bfloat16)
    mixing = jnp.concatenate([mixing, mixing], 1)
    mixing_high = mixing.astype(jnp.bfloat16)
    mixing_low = (mixing - mixing_high.astype(jnp.float32)).astype(jnp.bfloat16)
    mixing = jnp.concatenate([mixing_high, mixing_low], 0)

    sent = run_attend(queries, kv_cache, kv_new, lengths, parts, groups)
    gathered = lax.all_to_all(sent, EP, split_axis=0, concat_axis=0, tiled=True)
    columns = run_project(core_index, gathered.reshape(ep_size * row_count, depth), mine, other)
    terms = lax.all_to_all(
        columns.reshape(ep_size, row_count, parts * width), EP, split_axis=0, concat_axis=0, tiled=True
    )
    attn_out, normed = run_norm(terms, residual, norm_gain, parts)

    rows = jnp.concatenate([normed, swap(normed)], 0)
    outgoing = lax.dot_general(
        placing, rows, (((0,), (0,)), ((), ())), preferred_element_type=jnp.float32
    ).astype(jnp.bfloat16)
    arrived = lax.all_to_all(
        outgoing.reshape(chips, 2 * SLOTS, -1), CHIPS, split_axis=0, concat_axis=0, tiled=True
    )
    partial_value = run_expert(
        core_index,
        arrived.reshape(chips * 2 * SLOTS, -1),
        w_gate,
        w_up,
        w_down,
        gate_b,
        up_b,
        down_b,
    )
    returned = lax.all_to_all(
        partial_value.reshape(chips, 2 * SLOTS, -1), CHIPS, split_axis=0, concat_axis=0, tiled=True
    )
    mixed = jnp.dot(
        mixing, returned.reshape(chips * 2 * SLOTS, -1), preferred_element_type=jnp.float32
    )
    mixed = mixed[: 2 * row_count] + mixed[2 * row_count :]
    moe_out = mixed[:row_count] + swap(mixed[row_count:])
    return (attn_out, moe_out.astype(jnp.bfloat16))


def solution(mesh):
    fine = Mesh(mesh.devices.reshape(2, 2, 2, 2, 2, 4), ALL)
    return jax.shard_map(
        on_device,
        mesh=fine,
        in_specs=(
            P(ALL, None),
            P(ALL, None, None, None),
            P(ALL, None, None),
            P(ALL),
            P(ALL, None),
            P(),
            P(ALL, None),
            P(ALL, None),
            P(None, EP),
            P(EP, None, DP),
            P(EP, None, DP),
            P(EP, DP, None),
        ),
        out_specs=(P(ALL, None), P(ALL, None)),
        check_vma=False,
    )
```

```python
import functools
import math

import jax
import jax.numpy as jnp
from jax import lax
from jax.experimental import pallas as pl
from jax.experimental.pallas import tpu as pltpu
from jax.sharding import Mesh, PartitionSpec as P

HEADS = 64
KVH = 4
HD = 128
TOP = 8
SLOTS = 4

DP = ("xh", "core")
EP = ("xl", "yh", "yl", "z")
SPLIT = ("yl", "z")
CHIPS = ("xh",) + EP
ALL = DP + EP
SWAP = ((0, 1), (1, 0))
MIB = 1 << 20
BLOCK = 128
WIDE = 1024


def attend_kernel(lengths_ref, queries_ref, cache_hbm, fresh_ref, out_ref, cache, heads, sems, *, parts, copies):
    rows = queries_ref.shape[0]
    batch = rows // sems.shape[0]
    span = cache.shape[2]
    moves = []
    for number in range(sems.shape[0]):
        at = pl.ds(number * batch, batch)
        moves.append(pltpu.make_async_copy(cache_hbm.at[at], cache.at[at], sems.at[number]))
        moves[-1].start()
    groups = HEADS // KVH
    scaling = 1.0 / math.sqrt(HD)
    for head in range(HEADS):
        heads[pl.ds(head, rows, stride=HEADS), :] = queries_ref[:, head * HD : (head + 1) * HD].astype(jnp.float32)
    position = lax.broadcasted_iota(jnp.int32, (HEADS, span), 1)
    for row in range(rows):
        if row % batch == 0:
            moves[row // batch].wait()
        at = slice(row * HEADS, (row + 1) * HEADS)
        query = heads[at, :]
        query16 = query.astype(jnp.bfloat16)
        scores = []
        fresh = []
        for k in range(KVH):
            cols = slice(k * HD, (k + 1) * HD)
            own = slice(k * groups, (k + 1) * groups)
            scores.append(
                lax.dot_general(
                    query16[own], cache[row, 0, :, cols], (((1,), (1,)), ((), ())), preferred_element_type=jnp.float32
                )
            )
            key = fresh_ref[row, 0:1, cols].astype(jnp.float32)
            fresh.append(jnp.sum(query[own] * key, axis=1, keepdims=True))
        scores = jnp.concatenate(scores, 0) * scaling
        fresh = jnp.concatenate(fresh, 0) * scaling
        scores = jnp.where(position < lengths_ref[row], scores, -1e30)
        highest = jnp.maximum(jnp.max(scores, axis=1, keepdims=True), fresh)
        scores = jnp.exp(scores - highest)
        fresh = jnp.exp(fresh - highest)
        denominator = jnp.sum(scores, axis=1, keepdims=True) + fresh
        weights = (scores / denominator).astype(jnp.bfloat16)
        fresh = (fresh / denominator).astype(jnp.bfloat16).astype(jnp.float32)
        mixed = []
        for k in range(KVH):
            cols = slice(k * HD, (k + 1) * HD)
            own = slice(k * groups, (k + 1) * groups)
            value = jnp.dot(weights[own], cache[row, 1, :, cols], preferred_element_type=jnp.float32)
            mixed.append(value + fresh[own] * fresh_ref[row, 1:2, cols].astype(jnp.float32))
        heads[at, :] = jnp.concatenate(mixed, 0)
    share = HEADS // parts
    for head in range(HEADS):
        value = heads[pl.ds(head, rows, stride=HEADS), :].astype(jnp.bfloat16)
        cols = slice(head % share * HD, (head % share + 1) * HD)
        for copy in range(copies):
            out_ref[copy * parts + head // share, :, cols] = value

def run_attend(queries, kv_cache, kv_new, lengths, parts, copies):
    rows = queries.shape[0]
    return pl.pallas_call(
        functools.partial(attend_kernel, parts=parts, copies=copies),
        out_shape=pltpu.HBM((copies * parts, rows, HEADS * HD // parts), jnp.bfloat16),
        in_specs=[pl.BlockSpec(memory_space=pltpu.SMEM), pl.BlockSpec(memory_space=pltpu.VMEM), pl.BlockSpec(memory_space=pltpu.HBM), pl.BlockSpec(memory_space=pltpu.VMEM)],
        out_specs=pl.BlockSpec(memory_space=pltpu.VMEM),
        scratch_shapes=[pltpu.VMEM(kv_cache.shape, jnp.bfloat16), pltpu.VMEM((rows * HEADS, HD), jnp.float32), pltpu.SemaphoreType.DMA((4,))],
        compiler_params=pltpu.CompilerParams(vmem_limit_bytes=24 * MIB),
        cost_estimate=pl.CostEstimate(
            flops=4 * kv_cache.size // 2 * HEADS // KVH,
            bytes_accessed=2 * (kv_cache.size + 5 * queries.size),
            transcendentals=rows * HEADS * kv_cache.shape[2],
        ),
        name="attend",
    )(lengths, queries, pltpu.with_memory_space_constraint(kv_cache, pltpu.HBM), kv_new)


def expert_kernel(
    core_ref, rows_hbm, gate_a, up_a, down_a, gate_b, up_b, down_b, out_hbm, rows, gate, up, down, hidden, out, sems, out_sems
):
    mine = core_ref[0]
    count, depth = rows.shape
    share = gate.shape[2]
    moves = []

    def move(source, target):
        moves.append(pltpu.make_async_copy(source, target, sems.at[len(moves)]))
        return moves[-1:]

    def halves(source, target):
        size = target.shape[0] // 2
        found = []
        for half in range(2):
            at = pl.ds(half * size, size)
            found += move(source.at[at], target.at[at])
        return found

    def block_of(start):
        at = pl.ds(start, BLOCK)
        return move(gate_a.at[mine, :, at], gate.at[0, :, at]) + move(up_a.at[mine, :, at], up.at[0, :, at])

    def start_all(copies):
        for copy in copies:
            copy.start()

    def wait_all(copies):
        for copy in copies:
            copy.wait()

    def step(*places):
        @pl.when(mine >= 0)
        def _():
            for place, start in places:
                cols = slice(start, start + BLOCK)
                both = jnp.concatenate([gate[place, :, cols], up[place, :, cols]], axis=1)
                acts = jnp.dot(rows[...], both, preferred_element_type=jnp.float32)
                gate_act = acts[:, :BLOCK]
                value = gate_act / (1.0 + jnp.exp(-gate_act)) * acts[:, BLOCK:]
                at = place * share + start
                hidden[:, at : at + BLOCK] = value.astype(jnp.bfloat16)

    blocks = range(0, share, BLOCK)
    quarter = count // 4
    first = block_of(0)
    for part in range(4):
        at = pl.ds(part * quarter, quarter)
        first += move(rows_hbm.at[at], rows.at[at])
    second = [copy for start in blocks[1:] for copy in block_of(start)]
    third = halves(gate_b.at[mine], gate.at[1]) + halves(up_b.at[mine], up.at[1])
    last = halves(down_a.at[mine], down.at[0]) + halves(down_b.at[mine], down.at[1])
    start_all(first)
    wait_all(first)
    start_all(second + third)
    step((0, 0))
    wait_all(second)
    start_all(last)
    step(*((0, start) for start in blocks[1:]))
    wait_all(third)
    step(*((1, start) for start in blocks))
    wait_all(last)

    @pl.when(mine >= 0)
    def _():
        stores = []
        for start in range(0, depth, WIDE):
            cols = slice(start, start + WIDE)
            both = jnp.concatenate([down[0, :, cols], down[1, :, cols]], axis=0)
            out[:, cols] = jnp.dot(hidden[...], both, preferred_element_type=jnp.float32).astype(out.dtype)
            at = pl.ds(start, WIDE)
            stores.append(pltpu.make_async_copy(out.at[:, at], out_hbm.at[:, at], out_sems.at[start // WIDE]))
            stores[-1].start()
        wait_all(stores)


def run_expert(core, rows, gate_a, up_a, down_a, gate_b, up_b, down_b):
    count, depth = rows.shape
    share = gate_a.shape[2]
    hbm = pl.BlockSpec(memory_space=pltpu.HBM)
    return pl.pallas_call(
        expert_kernel,
        out_shape=pltpu.HBM((count, depth), jnp.bfloat16),
        in_specs=[pl.BlockSpec(memory_space=pltpu.SMEM)] + [hbm] * 7,
        out_specs=hbm,
        scratch_shapes=[
            pltpu.VMEM((count, depth), jnp.bfloat16),
            pltpu.VMEM((2, depth, share), jnp.bfloat16),
            pltpu.VMEM((2, depth, share), jnp.bfloat16),
            pltpu.VMEM((2, share, depth), jnp.bfloat16),
            pltpu.VMEM((count, 2 * share), jnp.bfloat16),
            pltpu.VMEM((count, depth), jnp.bfloat16),
            pltpu.SemaphoreType.DMA((4 + 2 * (share // BLOCK) + 8,)),
            pltpu.SemaphoreType.DMA((depth // WIDE,)),
        ],
        compiler_params=pltpu.CompilerParams(vmem_limit_bytes=48 * MIB),
        cost_estimate=pl.CostEstimate(
            flops=2 * count * depth * share * 6,
            bytes_accessed=2 * (2 * count * depth + 6 * depth * share),
            transcendentals=count * share * 2,
        ),
        name="expert",
    )(core, rows, gate_a, up_a, down_a, gate_b, up_b, down_b)


def project_kernel(core_ref, rows_ref, mine_ref, other_ref, out_ref):
    mine = core_ref[0]
    half = mine_ref.shape[1]
    width = mine_ref.shape[2]
    near = rows_ref[:, pl.ds(pl.multiple_of(mine * half, half), half)]
    far = rows_ref[:, pl.ds(pl.multiple_of((1 - mine) * half, half), half)]
    for block in range(0, mine_ref.shape[0], 2):
        weights = jnp.concatenate([mine_ref[block], mine_ref[block + 1]], axis=1)
        total = jnp.dot(near, weights, preferred_element_type=jnp.float32)
        weights = jnp.concatenate([other_ref[block], other_ref[block + 1]], axis=1)
        total += jnp.dot(far, weights, preferred_element_type=jnp.float32)
        out_ref[:, block * width : (block + 2) * width] = total.astype(out_ref.dtype)


def run_project(core, rows, mine, other):
    count, depth = rows.shape
    width = mine.shape[0] * mine.shape[2]
    vmem = pl.BlockSpec(memory_space=pltpu.VMEM)
    return pl.pallas_call(
        project_kernel,
        out_shape=jax.ShapeDtypeStruct((count, width), jnp.bfloat16),
        in_specs=[pl.BlockSpec(memory_space=pltpu.SMEM)] + [vmem] * 3,
        out_specs=vmem,
        compiler_params=pltpu.CompilerParams(vmem_limit_bytes=16 * MIB),
        cost_estimate=pl.CostEstimate(
            flops=2 * count * depth * width,
            bytes_accessed=2 * (count * depth + count * width + depth * width),
            transcendentals=0,
        ),
        name="project",
    )(core, rows, mine, other)


def norm_kernel(terms_ref, residual_ref, gain_ref, out_ref, normed_ref, *, parts):
    width = terms_ref.shape[2]
    streams = []
    squares = None
    for group in range(terms_ref.shape[0] // parts):
        cols = slice(group * width, (group + 1) * width)
        total = terms_ref[group * parts].astype(jnp.float32)
        for part in range(1, parts):
            total += terms_ref[group * parts + part].astype(jnp.float32)
        total = total.astype(jnp.bfloat16)
        out_ref[:, cols] = total
        stream = residual_ref[:, cols].astype(jnp.float32) + total.astype(jnp.float32)
        square = jnp.sum(stream * stream, axis=1, keepdims=True)
        squares = square if squares is None else squares + square
        streams.append(stream)
    scale = lax.rsqrt(squares / out_ref.shape[1] + 1e-06)
    for group, stream in enumerate(streams):
        cols = slice(group * width, (group + 1) * width)
        normed_ref[:, cols] = (stream * scale * gain_ref[:, cols]).astype(jnp.bfloat16)


def run_norm(terms, residual, gain, parts):
    vmem = pl.BlockSpec(memory_space=pltpu.VMEM)
    return pl.pallas_call(
        functools.partial(norm_kernel, parts=parts),
        out_shape=[jax.ShapeDtypeStruct(residual.shape, jnp.bfloat16)] * 2,
        in_specs=[vmem] * 3,
        out_specs=[vmem] * 2,
        compiler_params=pltpu.CompilerParams(vmem_limit_bytes=16 * MIB),
        cost_estimate=pl.CostEstimate(
            flops=2 * terms.size, bytes_accessed=2 * terms.size, transcendentals=0
        ),
        name="norm",
    )(terms, residual, gain.reshape(1, -1))


def place_kernel(placing_ref, own_ref, other_ref, out_hbm, out, sems):
    count = placing_ref.shape[0]
    step = count // 4
    rows = jnp.concatenate([own_ref[...], other_ref[...]], axis=0)
    stores = []
    for start in range(0, count, step):
        value = jnp.dot(placing_ref[start : start + step, :], rows, preferred_element_type=jnp.float32)
        out[start : start + step, :] = value.astype(out.dtype)
        for copy in range(2):
            stores.append(
                pltpu.make_async_copy(
                    out.at[pl.ds(start, step)],
                    out_hbm.at[pl.ds(copy * count + start, step)],
                    sems.at[len(stores)],
                )
            )
            stores[-1].start()
    for store in stores:
        store.wait()


def run_place(placing, own, other):
    vmem = pl.BlockSpec(memory_space=pltpu.VMEM)
    count, depth = placing.shape[0], own.shape[1]
    return pl.pallas_call(
        place_kernel,
        out_shape=pltpu.HBM((2 * count, depth), jnp.bfloat16),
        in_specs=[vmem] * 3,
        out_specs=pl.BlockSpec(memory_space=pltpu.HBM),
        scratch_shapes=[pltpu.VMEM((count, depth), jnp.bfloat16), pltpu.SemaphoreType.DMA((8,))],
        compiler_params=pltpu.CompilerParams(vmem_limit_bytes=16 * MIB),
        cost_estimate=pl.CostEstimate(
            flops=2 * placing.size * depth, bytes_accessed=4 * count * depth, transcendentals=0
        ),
        name="place",
    )(placing, own, other)


def swap(value):
    return lax.ppermute(value, "core", SWAP)


def places(expert_ids, core, expert_total):
    row_count = expert_ids.shape[0]
    pair_ids = expert_ids.reshape(-1)
    member = (pair_ids[:, None] == jnp.arange(expert_total, dtype=jnp.int32)[None, :]).astype(
        jnp.int32
    )
    ranking = jnp.sum((jnp.cumsum(member, 0) - 1) * member, 1)
    here = (pair_ids % 2) == core
    slot = (pair_ids // 2) * (2 * SLOTS) + ranking
    slot = jnp.where(here, slot, -1)
    return slot.reshape(row_count, TOP)


def on_device(
    queries,
    kv_cache,
    kv_new,
    lengths,
    residual,
    norm_gain,
    expert_ids,
    route_probs,
    w_out,
    w_gate,
    w_up,
    w_down,
):
    row_count = queries.shape[0]
    core = lax.axis_index("core")
    core_index = core.astype(jnp.int32).reshape(1)
    ep_size = lax.axis_size(EP)
    parts = lax.axis_size(SPLIT)
    groups = ep_size // parts
    chips = lax.axis_size(CHIPS)
    depth = w_out.shape[0] // parts
    half = depth // 2
    width = w_out.shape[1]

    mine = lax.dynamic_index_in_dim(
        w_out.reshape(parts, 2, half, width), core, axis=1, keepdims=False
    )
    mine = lax.all_to_all(mine, SPLIT, split_axis=0, concat_axis=0, tiled=True)

    gate_b, up_b, down_b = swap(w_gate), swap(w_up), swap(w_down)

    expert_total = w_gate.shape[0] * ep_size
    slot_total = 2 * SLOTS * ep_size
    gates = route_probs / jnp.sum(route_probs, -1, keepdims=True)
    own_slots = places(expert_ids, core, expert_total)
    other_slots = places(swap(expert_ids), core, expert_total)
    other_slots = jnp.where(other_slots >= 0, other_slots + SLOTS, -1)
    slots = jnp.concatenate([own_slots, other_slots], 0)
    both_gates = jnp.concatenate([gates, swap(gates)], 0)
    chosen = slots[:, :, None] == jnp.arange(slot_total, dtype=jnp.int32)[None, None, :]
    placing = jnp.any(chosen, 1)
    mixing = jnp.sum(jnp.where(chosen, both_gates[:, :, None], 0.0), 1)
    placing = placing.astype(jnp.bfloat16).T
    mixing = jnp.concatenate([mixing, mixing], 1)
    mixing_high = mixing.astype(jnp.bfloat16)
    mixing_low = (mixing - mixing_high.astype(jnp.float32)).astype(jnp.bfloat16)
    mixing = jnp.concatenate([mixing_high, mixing_low], 0)

    sent = run_attend(queries, kv_cache, kv_new, lengths, parts, groups)
    sent, mine = lax.optimization_barrier((sent, mine))
    gathered = lax.all_to_all(sent, EP, split_axis=0, concat_axis=0, tiled=True)
    other = swap(mine)
    columns = run_project(core_index, gathered.reshape(ep_size * row_count, depth), mine, other)
    terms = lax.all_to_all(
        columns.reshape(ep_size, row_count, parts * width), EP, split_axis=0, concat_axis=0, tiled=True
    )
    attn_out, normed = run_norm(terms, residual, norm_gain, parts)

    outgoing = run_place(placing, normed, swap(normed))
    arrived = lax.all_to_all(
        outgoing.reshape(chips, 2 * SLOTS, -1), CHIPS, split_axis=0, concat_axis=0, tiled=True
    )
    partial_value = run_expert(
        core_index,
        arrived.reshape(chips * 2 * SLOTS, -1),
        w_gate,
        w_up,
        w_down,
        gate_b,
        up_b,
        down_b,
    )
    returned = lax.all_to_all(
        partial_value.reshape(chips, 2 * SLOTS, -1), CHIPS, split_axis=0, concat_axis=0, tiled=True
    )
    mixed = jnp.dot(
        mixing, returned.reshape(chips * 2 * SLOTS, -1), preferred_element_type=jnp.float32
    )
    mixed = mixed[: 2 * row_count] + mixed[2 * row_count :]
    moe_out = mixed[:row_count] + swap(mixed[row_count:].astype(jnp.bfloat16)).astype(jnp.float32)
    return (attn_out, moe_out.astype(jnp.bfloat16))


def solution(mesh):
    fine = Mesh(mesh.devices.reshape(2, 2, 2, 2, 2, 4), ALL)
    return jax.shard_map(
        on_device,
        mesh=fine,
        in_specs=(
            P(ALL, None),
            P(ALL, None, None, None),
            P(ALL, None, None),
            P(ALL),
            P(ALL, None),
            P(),
            P(ALL, None),
            P(ALL, None),
            P(None, EP),
            P(EP, None, DP),
            P(EP, None, DP),
            P(EP, DP, None),
        ),
        out_specs=(P(ALL, None), P(ALL, None)),
        check_vma=False,
    )
```

```python
import functools
import math

import jax
import jax.numpy as jnp
from jax import lax
from jax.experimental import pallas as pl
from jax.experimental.pallas import tpu as pltpu
from jax.sharding import Mesh, PartitionSpec as P

HEADS = 64
KVH = 4
HD = 128
TOP = 8
SLOTS = 4

DP = ("xh", "core")
EP = ("xl", "yh", "yl", "z")
PLANE = ("xh", "xl", "yh", "yl")
CHIPS = ("xh",) + EP
ALL = DP + EP
SWAP = ((0, 1), (1, 0))
MIB = 1 << 20
BLOCK = 128
WIDE = 1024


def attend_kernel(
    lengths_ref, queries_hbm, cache_hbm, fresh_hbm, out_ref, queries_ref, cache, fresh_ref, heads, sems, *, parts, copies
):
    rows = queries_ref.shape[0]
    batches = sems.shape[0] - 2
    batch = rows // batches
    span = cache.shape[2]
    others = [
        pltpu.make_async_copy(queries_hbm, queries_ref, sems.at[batches]),
        pltpu.make_async_copy(fresh_hbm, fresh_ref, sems.at[batches + 1]),
    ]
    for other in others:
        other.start()
    moves = []
    for number in range(batches):
        at = pl.ds(number * batch, batch)
        moves.append(pltpu.make_async_copy(cache_hbm.at[at], cache.at[at], sems.at[number]))
        moves[-1].start()
    groups = HEADS // KVH
    scaling = 1.0 / math.sqrt(HD)
    for other in others:
        other.wait()
    for head in range(HEADS):
        query = queries_ref[:, head * HD : (head + 1) * HD].astype(jnp.float32)
        heads[pl.ds(head, rows, stride=HEADS), :] = query
    position = lax.broadcasted_iota(jnp.int32, (HEADS, span), 1)
    for number, move in enumerate(moves):
        move.wait()
        those = range(number * batch, (number + 1) * batch)
        at = slice(number * batch * HEADS, (number + 1) * batch * HEADS)
        query = heads[at, :]
        rounded = query.astype(jnp.bfloat16)
        blocks = [
            (row, kv, slice(kv * HD, (kv + 1) * HD), slice(place * groups, (place + 1) * groups))
            for place, (row, kv) in enumerate((row, kv) for row in those for kv in range(KVH))
        ]
        scores = jnp.concatenate(
            [
                lax.dot_general(
                    rounded[own], cache[row, 0, :, cols], (((1,), (1,)), ((), ())), preferred_element_type=jnp.float32
                )
                for row, kv, cols, own in blocks
            ],
            axis=0,
        )
        keys = [
            jnp.broadcast_to(fresh_ref[row, 0:1, cols].astype(jnp.float32), (groups, HD)) for row, kv, cols, own in blocks
        ]
        fresh = jnp.sum(query * jnp.concatenate(keys, axis=0), axis=1, keepdims=True) * scaling
        live = jnp.concatenate([position < lengths_ref[row] for row in those], axis=0)
        scores = jnp.where(live, scores * scaling, -1e30)
        highest = jnp.maximum(jnp.max(scores, axis=1, keepdims=True), fresh)
        scores = jnp.exp(scores - highest)
        fresh = jnp.exp(fresh - highest)
        denominator = jnp.sum(scores, axis=1, keepdims=True) + fresh
        weights = (scores / denominator).astype(jnp.bfloat16)
        fresh = (fresh / denominator).astype(jnp.bfloat16).astype(jnp.float32)
        mixed = [
            jnp.dot(weights[own], cache[row, 1, :, cols], preferred_element_type=jnp.float32)
            + fresh[own] * fresh_ref[row, 1:2, cols].astype(jnp.float32)
            for row, kv, cols, own in blocks
        ]
        heads[at, :] = jnp.concatenate(mixed, axis=0)
    share = HEADS // parts
    for head in range(HEADS):
        value = heads[pl.ds(head, rows, stride=HEADS), :].astype(jnp.bfloat16)
        cols = slice(head % share * HD, (head % share + 1) * HD)
        outer, inner = divmod(head // share, 2)
        for copy in range(copies):
            out_ref[(outer * copies + copy) * 2 + inner, :, cols] = value

def run_attend(queries, kv_cache, kv_new, lengths, parts, copies):
    rows = queries.shape[0]
    hbm = pl.BlockSpec(memory_space=pltpu.HBM)
    operands = [pltpu.with_memory_space_constraint(value, pltpu.HBM) for value in (queries, kv_cache, kv_new)]
    return pl.pallas_call(
        functools.partial(attend_kernel, parts=parts, copies=copies),
        out_shape=pltpu.HBM((copies * parts, rows, HEADS * HD // parts), jnp.bfloat16),
        in_specs=[pl.BlockSpec(memory_space=pltpu.SMEM)] + [hbm] * 3,
        out_specs=pl.BlockSpec(memory_space=pltpu.VMEM),
        scratch_shapes=[
            pltpu.VMEM(queries.shape, jnp.bfloat16),
            pltpu.VMEM(kv_cache.shape, jnp.bfloat16),
            pltpu.VMEM(kv_new.shape, jnp.bfloat16),
            pltpu.VMEM((rows * HEADS, HD), jnp.float32),
            pltpu.SemaphoreType.DMA((6,)),
        ],
        compiler_params=pltpu.CompilerParams(vmem_limit_bytes=24 * MIB),
        cost_estimate=pl.CostEstimate(
            flops=4 * kv_cache.size // 2 * HEADS // KVH,
            bytes_accessed=2 * (kv_cache.size + 5 * queries.size),
            transcendentals=rows * HEADS * kv_cache.shape[2],
        ),
        name="attend",
    )(lengths, *operands)


def expert_kernel(
    core_ref, rows, gate_a, up_a, down_a, gate_b, up_b, down_b, out_hbm, gate, up, down, hidden, out, sems, out_sems
):
    mine = core_ref[0]
    depth = rows.shape[1]
    share = gate.shape[1]
    moves = []
    for source, target in ((gate_a, gate), (up_a, up), (down_a, down)):
        size = target.shape[0] // 2
        for half in range(2):
            at = pl.ds(half * size, size)
            moves.append(pltpu.make_async_copy(source.at[mine, at], target.at[at], sems.at[len(moves)]))
            moves[-1].start()

    def step(gate_of, up_of, base):
        @pl.when(mine >= 0)
        def _():
            for start in range(0, share, BLOCK):
                cols = slice(start, start + BLOCK)
                both = jnp.concatenate([gate_of(cols), up_of(cols)], axis=1)
                acts = jnp.dot(rows[...], both, preferred_element_type=jnp.float32)
                gate_act = acts[:, :BLOCK]
                value = gate_act / (1.0 + jnp.exp(-gate_act)) * acts[:, BLOCK:]
                hidden[:, base + start : base + start + BLOCK] = value.astype(jnp.bfloat16)

    step(lambda cols: gate_b[mine, :, cols], lambda cols: up_b[mine, :, cols], 0)
    for move in moves[:4]:
        move.wait()
    step(lambda cols: gate[:, cols], lambda cols: up[:, cols], share)
    for move in moves[4:]:
        move.wait()

    @pl.when(mine >= 0)
    def _():
        stores = []
        for start in range(0, depth, WIDE):
            cols = slice(start, start + WIDE)
            both = jnp.concatenate([down_b[mine, :, cols], down[:, cols]], axis=0)
            out[:, cols] = jnp.dot(hidden[...], both, preferred_element_type=jnp.float32).astype(out.dtype)
            at = pl.ds(start, WIDE)
            stores.append(pltpu.make_async_copy(out.at[:, at], out_hbm.at[:, at], out_sems.at[start // WIDE]))
            stores[-1].start()
        for store in stores:
            store.wait()


def run_expert(core, rows, gate_a, up_a, down_a, gate_b, up_b, down_b):
    count, depth = rows.shape
    share = gate_a.shape[2]
    hbm = pl.BlockSpec(memory_space=pl.ANY)
    vmem = pl.BlockSpec(memory_space=pltpu.VMEM)
    rows, gate_b, up_b, down_b = (
        pltpu.with_memory_space_constraint(value, pltpu.VMEM) for value in (rows, gate_b, up_b, down_b)
    )
    return pl.pallas_call(
        expert_kernel,
        out_shape=pltpu.HBM((count, depth), jnp.bfloat16),
        in_specs=[pl.BlockSpec(memory_space=pltpu.SMEM), vmem] + [hbm] * 3 + [vmem] * 3,
        out_specs=hbm,
        scratch_shapes=[
            pltpu.VMEM((depth, share), jnp.bfloat16),
            pltpu.VMEM((depth, share), jnp.bfloat16),
            pltpu.VMEM((share, depth), jnp.bfloat16),
            pltpu.VMEM((count, 2 * share), jnp.bfloat16),
            pltpu.VMEM((count, depth), jnp.bfloat16),
            pltpu.SemaphoreType.DMA((6,)),
            pltpu.SemaphoreType.DMA((depth // WIDE,)),
        ],
        compiler_params=pltpu.CompilerParams(vmem_limit_bytes=24 * MIB),
        cost_estimate=pl.CostEstimate(
            flops=2 * count * depth * share * 6,
            bytes_accessed=2 * (2 * count * depth + 6 * depth * share),
            transcendentals=count * share * 2,
        ),
        name="expert",
    )(core, rows, gate_a, up_a, down_a, gate_b, up_b, down_b)


def project_kernel(place_ref, rows_ref, *refs):
    *weights, out_ref = refs
    half, width = weights[0].shape[1:]
    ring = len(weights) // 2
    pair, turn, core = place_ref[0], place_ref[1], place_ref[2]
    near = rows_ref[:, pl.ds(pl.multiple_of(core * half, half), half)]
    far = rows_ref[:, pl.ds(pl.multiple_of((1 - core) * half, half), half)]
    for step in range(ring):
        total = None
        for rows, weight in ((near, weights[step]), (far, weights[ring + step])):
            both = jnp.concatenate([weight[0], weight[1]], axis=1)
            term = jnp.dot(rows, both, preferred_element_type=jnp.float32)
            total = term if total is None else total + term
        total = total.astype(out_ref.dtype)
        for which in range(2):
            owner = (pair + which) % 2 * ring + (turn + ring - step) % ring
            cols = pl.ds(pl.multiple_of(owner * width, width), width)
            out_ref[:, cols] = total[:, which * width : (which + 1) * width]


def run_project(place, rows, weights):
    count, depth = rows.shape
    width = len(weights) * weights[0].shape[2]
    vmem = pl.BlockSpec(memory_space=pltpu.VMEM)
    return pl.pallas_call(
        project_kernel,
        out_shape=pltpu.HBM((count, width), jnp.bfloat16),
        in_specs=[pl.BlockSpec(memory_space=pltpu.SMEM)] + [vmem] * (1 + len(weights)),
        out_specs=vmem,
        compiler_params=pltpu.CompilerParams(vmem_limit_bytes=16 * MIB),
        cost_estimate=pl.CostEstimate(
            flops=2 * count * depth * width,
            bytes_accessed=2 * (count * depth + count * width + depth * width),
            transcendentals=0,
        ),
        name="project",
    )(place, rows, *weights)


def norm_kernel(terms_ref, residual_ref, gain_ref, out_ref, normed_ref, *, parts):
    width = terms_ref.shape[2]
    streams = []
    squares = None
    groups = terms_ref.shape[0] // parts
    outer = parts // 2
    for group in range(groups):
        cols = slice(group * width, (group + 1) * width)
        total = None
        for part in range(outer):
            for inner in range(2):
                term = terms_ref[(part * groups + group) * 2 + inner].astype(jnp.float32)
                total = term if total is None else total + term
        total = total.astype(jnp.bfloat16)
        out_ref[:, cols] = total
        stream = residual_ref[:, cols].astype(jnp.float32) + total.astype(jnp.float32)
        square = jnp.sum(stream * stream, axis=1, keepdims=True)
        squares = square if squares is None else squares + square
        streams.append(stream)
    scale = lax.rsqrt(squares / out_ref.shape[1] + 1e-06)
    for group, stream in enumerate(streams):
        cols = slice(group * width, (group + 1) * width)
        normed_ref[:, cols] = (stream * scale * gain_ref[:, cols]).astype(jnp.bfloat16)


def run_norm(terms, residual, gain, parts):
    vmem = pl.BlockSpec(memory_space=pltpu.VMEM)
    return pl.pallas_call(
        functools.partial(norm_kernel, parts=parts),
        out_shape=[jax.ShapeDtypeStruct(residual.shape, jnp.bfloat16)] * 2,
        in_specs=[vmem] * 3,
        out_specs=[vmem] * 2,
        compiler_params=pltpu.CompilerParams(vmem_limit_bytes=16 * MIB),
        cost_estimate=pl.CostEstimate(
            flops=2 * terms.size, bytes_accessed=2 * terms.size, transcendentals=0
        ),
        name="norm",
    )(terms, residual, gain.reshape(1, -1))


def place_kernel(placing_ref, own_ref, other_ref, out_hbm, out, sems):
    count = placing_ref.shape[0]
    step = count // 4
    rows = jnp.concatenate([own_ref[...], other_ref[...]], axis=0)
    stores = []
    for start in range(0, count, step):
        value = jnp.dot(placing_ref[start : start + step, :], rows, preferred_element_type=jnp.float32)
        out[start : start + step, :] = value.astype(out.dtype)
        for copy in range(2):
            stores.append(
                pltpu.make_async_copy(
                    out.at[pl.ds(start, step)],
                    out_hbm.at[pl.ds(copy * count + start, step)],
                    sems.at[len(stores)],
                )
            )
            stores[-1].start()
    for store in stores:
        store.wait()


def run_place(placing, own, other):
    vmem = pl.BlockSpec(memory_space=pltpu.VMEM)
    count, depth = placing.shape[0], own.shape[1]
    return pl.pallas_call(
        place_kernel,
        out_shape=pltpu.HBM((2 * count, depth), jnp.bfloat16),
        in_specs=[vmem] * 3,
        out_specs=pl.BlockSpec(memory_space=pltpu.HBM),
        scratch_shapes=[pltpu.VMEM((count, depth), jnp.bfloat16), pltpu.SemaphoreType.DMA((8,))],
        compiler_params=pltpu.CompilerParams(vmem_limit_bytes=16 * MIB),
        cost_estimate=pl.CostEstimate(
            flops=2 * placing.size * depth, bytes_accessed=4 * count * depth, transcendentals=0
        ),
        name="place",
    )(placing, own, other)


def swap(value):
    return lax.ppermute(value, "core", SWAP)


def places(expert_ids, core, expert_total):
    row_count = expert_ids.shape[0]
    pair_ids = expert_ids.reshape(-1)
    member = (pair_ids[:, None] == jnp.arange(expert_total, dtype=jnp.int32)[None, :]).astype(
        jnp.int32
    )
    ranking = jnp.sum((jnp.cumsum(member, 0) - 1) * member, 1)
    here = (pair_ids % 2) == core
    slot = (pair_ids // 2) * (2 * SLOTS) + ranking
    slot = jnp.where(here, slot, -1)
    return slot.reshape(row_count, TOP)


def on_device(
    queries,
    kv_cache,
    kv_new,
    lengths,
    residual,
    norm_gain,
    expert_ids,
    route_probs,
    w_out,
    w_gate,
    w_up,
    w_down,
):
    row_count = queries.shape[0]
    core = lax.axis_index("core")
    core_index = core.astype(jnp.int32).reshape(1)
    ep_size = lax.axis_size(EP)
    plane = lax.axis_size(PLANE)
    chips = lax.axis_size(CHIPS)
    ring = lax.axis_size("z")
    parts = 2 * lax.axis_size("xh")
    depth = w_out.shape[0] // parts
    half = depth // 2

    pair = lax.axis_index("yl")
    quarter = lax.axis_index("xh") * 2
    kept = lax.dynamic_slice_in_dim(w_out, (quarter + pair) * depth + core * half, half, axis=0)
    given = lax.dynamic_slice_in_dim(w_out, (quarter + 1 - pair) * depth + core * half, half, axis=0)
    taken = lax.ppermute(given, "yl", SWAP)
    sent = run_attend(queries, kv_cache, kv_new, lengths, parts, plane // parts)
    sent, taken, expert_ids, route_probs = lax.optimization_barrier((sent, taken, expert_ids, route_probs))
    weights = [jnp.stack([kept, taken])]
    for step in range(1, ring):
        turn = [(place, (place + step) % ring) for place in range(ring)]
        weights.append(lax.ppermute(weights[0], "z", turn))
    weights += [swap(value) for value in weights]
    place = jnp.stack([pair, lax.axis_index("z"), core]).astype(jnp.int32)

    expert_total = w_gate.shape[0] * ep_size
    slot_total = 2 * SLOTS * ep_size
    gates = route_probs / jnp.sum(route_probs, -1, keepdims=True)
    own_slots = places(expert_ids, core, expert_total)
    other_slots = places(swap(expert_ids), core, expert_total)
    other_slots = jnp.where(other_slots >= 0, other_slots + SLOTS, -1)
    slots = jnp.concatenate([own_slots, other_slots], 0)
    both_gates = jnp.concatenate([gates, swap(gates)], 0)
    chosen = slots[:, :, None] == jnp.arange(slot_total, dtype=jnp.int32)[None, None, :]
    placing = jnp.any(chosen, 1)
    mixing = jnp.sum(jnp.where(chosen, both_gates[:, :, None], 0.0), 1)
    placing = placing.astype(jnp.bfloat16).T
    mixing = jnp.concatenate([mixing, mixing], 1)
    mixing_high = mixing.astype(jnp.bfloat16)
    mixing_low = (mixing - mixing_high.astype(jnp.float32)).astype(jnp.bfloat16)
    mixing = jnp.concatenate([mixing_high, mixing_low], 0)

    gathered = lax.all_to_all(sent, PLANE, split_axis=0, concat_axis=0, tiled=True)
    columns = run_project(place, gathered.reshape(plane * row_count, depth), weights)
    columns, placing, mixing = lax.optimization_barrier((columns, placing, mixing))
    terms = lax.all_to_all(
        columns.reshape(plane, row_count, -1), PLANE, split_axis=0, concat_axis=0, tiled=True
    )
    attn_out, normed = run_norm(terms, residual, norm_gain, parts)

    other_normed = swap(normed)
    other_normed, w_gate, w_up, w_down = lax.optimization_barrier((other_normed, w_gate, w_up, w_down))
    gate_b, up_b, down_b = swap(w_gate), swap(w_up), swap(w_down)
    outgoing = run_place(placing, normed, other_normed)
    arrived = lax.all_to_all(
        outgoing.reshape(chips, 2 * SLOTS, -1), CHIPS, split_axis=0, concat_axis=0, tiled=True
    )
    partial_value = run_expert(
        core_index,
        arrived.reshape(chips * 2 * SLOTS, -1),
        w_gate,
        w_up,
        w_down,
        gate_b,
        up_b,
        down_b,
    )
    returned = lax.all_to_all(
        partial_value.reshape(chips, 2 * SLOTS, -1), CHIPS, split_axis=0, concat_axis=0, tiled=True
    )
    mixed = jnp.dot(
        mixing, returned.reshape(chips * 2 * SLOTS, -1), preferred_element_type=jnp.float32
    )
    mixed = mixed[: 2 * row_count] + mixed[2 * row_count :]
    moe_out = mixed[:row_count] + swap(mixed[row_count:].astype(jnp.bfloat16)).astype(jnp.float32)
    return (attn_out, moe_out.astype(jnp.bfloat16))


def solution(mesh):
    fine = Mesh(mesh.devices.reshape(2, 2, 2, 2, 2, 4), ALL)
    return jax.shard_map(
        on_device,
        mesh=fine,
        in_specs=(
            P(ALL, None),
            P(ALL, None, None, None),
            P(ALL, None, None),
            P(ALL),
            P(ALL, None),
            P(),
            P(ALL, None),
            P(ALL, None),
            P(None, EP),
            P(EP, None, DP),
            P(EP, None, DP),
            P(EP, DP, None),
        ),
        out_specs=(P(ALL, None), P(ALL, None)),
        check_vma=False,
    )
```

```python
import functools
import math

import jax
import jax.numpy as jnp
from jax import lax
from jax.experimental import pallas as pl
from jax.experimental.pallas import tpu as pltpu
from jax.sharding import Mesh, PartitionSpec as P

HEADS = 64
KVH = 4
HD = 128
TOP = 8
SLOTS = 4

DP = ("xh", "core")
EP = ("xl", "yh", "yl", "z")
PLANE = ("xh", "xl", "yh", "yl")
CHIPS = ("xh",) + EP
ALL = DP + EP
SWAP = ((0, 1), (1, 0))
MIB = 1 << 20
BLOCK = 128
WIDE = 1024


def attend_kernel(
    lengths_hbm, queries_hbm, cache_hbm, fresh_hbm, out_ref, lengths_ref, queries_ref, cache, fresh_ref, heads, sems, *, parts, copies
):
    rows = queries_ref.shape[0]
    batches = sems.shape[0] - 3
    batch = rows // batches
    span = cache.shape[2]
    others = [
        pltpu.make_async_copy(queries_hbm, queries_ref, sems.at[batches]),
        pltpu.make_async_copy(fresh_hbm, fresh_ref, sems.at[batches + 1]),
        pltpu.make_async_copy(lengths_hbm, lengths_ref, sems.at[batches + 2]),
    ]
    for other in others:
        other.start()
    moves = []
    for number in range(batches):
        at = pl.ds(number * batch, batch)
        moves.append(pltpu.make_async_copy(cache_hbm.at[at], cache.at[at], sems.at[number]))
        moves[-1].start()
    groups = HEADS // KVH
    scaling = 1.0 / math.sqrt(HD)
    for other in others:
        other.wait()
    for head in range(HEADS):
        query = queries_ref[:, head * HD : (head + 1) * HD].astype(jnp.float32)
        heads[pl.ds(head, rows, stride=HEADS), :] = query
    position = lax.broadcasted_iota(jnp.int32, (HEADS, span), 1)
    for number, move in enumerate(moves):
        move.wait()
        those = range(number * batch, (number + 1) * batch)
        at = slice(number * batch * HEADS, (number + 1) * batch * HEADS)
        query = heads[at, :]
        rounded = query.astype(jnp.bfloat16)
        blocks = [
            (row, kv, slice(kv * HD, (kv + 1) * HD), slice(place * groups, (place + 1) * groups))
            for place, (row, kv) in enumerate((row, kv) for row in those for kv in range(KVH))
        ]
        scores = jnp.concatenate(
            [
                lax.dot_general(
                    rounded[own], cache[row, 0, :, cols], (((1,), (1,)), ((), ())), preferred_element_type=jnp.float32
                )
                for row, kv, cols, own in blocks
            ],
            axis=0,
        )
        keys = [
            jnp.broadcast_to(fresh_ref[row, 0:1, cols].astype(jnp.float32), (groups, HD)) for row, kv, cols, own in blocks
        ]
        fresh = jnp.sum(query * jnp.concatenate(keys, axis=0), axis=1, keepdims=True) * scaling
        live = jnp.concatenate([position < lengths_ref[row] for row in those], axis=0)
        scores = jnp.where(live, scores * scaling, -1e30)
        highest = jnp.maximum(jnp.max(scores, axis=1, keepdims=True), fresh)
        scores = jnp.exp(scores - highest)
        fresh = jnp.exp(fresh - highest)
        denominator = jnp.sum(scores, axis=1, keepdims=True) + fresh
        weights = (scores / denominator).astype(jnp.bfloat16)
        fresh = (fresh / denominator).astype(jnp.bfloat16).astype(jnp.float32)
        mixed = [
            jnp.dot(weights[own], cache[row, 1, :, cols], preferred_element_type=jnp.float32)
            + fresh[own] * fresh_ref[row, 1:2, cols].astype(jnp.float32)
            for row, kv, cols, own in blocks
        ]
        heads[at, :] = jnp.concatenate(mixed, axis=0)
    share = HEADS // parts
    for head in range(HEADS):
        value = heads[pl.ds(head, rows, stride=HEADS), :].astype(jnp.bfloat16)
        cols = slice(head % share * HD, (head % share + 1) * HD)
        outer, inner = divmod(head // share, 2)
        for copy in range(copies):
            out_ref[(outer * copies + copy) * 2 + inner, :, cols] = value

def run_attend(queries, kv_cache, kv_new, lengths, parts, copies):
    rows = queries.shape[0]
    hbm = pl.BlockSpec(memory_space=pltpu.HBM)
    operands = [pltpu.with_memory_space_constraint(value, pltpu.HBM) for value in (lengths, queries, kv_cache, kv_new)]
    return pl.pallas_call(
        functools.partial(attend_kernel, parts=parts, copies=copies),
        out_shape=pltpu.HBM((copies * parts, rows, HEADS * HD // parts), jnp.bfloat16),
        in_specs=[hbm] * 4,
        out_specs=pl.BlockSpec(memory_space=pltpu.VMEM),
        scratch_shapes=[
            pltpu.SMEM(lengths.shape, jnp.int32),
            pltpu.VMEM(queries.shape, jnp.bfloat16),
            pltpu.VMEM(kv_cache.shape, jnp.bfloat16),
            pltpu.VMEM(kv_new.shape, jnp.bfloat16),
            pltpu.VMEM((rows * HEADS, HD), jnp.float32),
            pltpu.SemaphoreType.DMA((7,)),
        ],
        compiler_params=pltpu.CompilerParams(vmem_limit_bytes=24 * MIB),
        cost_estimate=pl.CostEstimate(
            flops=4 * kv_cache.size // 2 * HEADS // KVH,
            bytes_accessed=2 * (kv_cache.size + 5 * queries.size),
            transcendentals=rows * HEADS * kv_cache.shape[2],
        ),
        name="attend",
    )(*operands)


def expert_kernel(
    core_ref, rows, gate_a, up_a, down_a, gate_b, up_b, down_b, out, gate, up, down, hidden, sems
):
    mine = core_ref[0]
    depth = rows.shape[1]
    share = gate.shape[1]
    moves = []
    for source, target in ((gate_a, gate), (up_a, up), (down_a, down)):
        size = target.shape[0] // 2
        for half in range(2):
            at = pl.ds(half * size, size)
            moves.append(pltpu.make_async_copy(source.at[mine, at], target.at[at], sems.at[len(moves)]))
            moves[-1].start()

    def step(gate_of, up_of, base):
        @pl.when(mine >= 0)
        def _():
            for start in range(0, share, BLOCK):
                cols = slice(start, start + BLOCK)
                both = jnp.concatenate([gate_of(cols), up_of(cols)], axis=1)
                acts = jnp.dot(rows[...], both, preferred_element_type=jnp.float32)
                gate_act = acts[:, :BLOCK]
                value = gate_act / (1.0 + jnp.exp(-gate_act)) * acts[:, BLOCK:]
                hidden[:, base + start : base + start + BLOCK] = value.astype(jnp.bfloat16)

    step(lambda cols: gate_b[mine, :, cols], lambda cols: up_b[mine, :, cols], 0)
    for move in moves[:4]:
        move.wait()
    step(lambda cols: gate[:, cols], lambda cols: up[:, cols], share)
    for move in moves[4:]:
        move.wait()

    @pl.when(mine >= 0)
    def _():
        for start in range(0, depth, WIDE):
            cols = slice(start, start + WIDE)
            both = jnp.concatenate([down_b[mine, :, cols], down[:, cols]], axis=0)
            out[:, cols] = jnp.dot(hidden[...], both, preferred_element_type=jnp.float32).astype(out.dtype)


def run_expert(core, rows, gate_a, up_a, down_a, gate_b, up_b, down_b):
    count, depth = rows.shape
    share = gate_a.shape[2]
    hbm = pl.BlockSpec(memory_space=pl.ANY)
    vmem = pl.BlockSpec(memory_space=pltpu.VMEM)
    rows, gate_b, up_b, down_b = (
        pltpu.with_memory_space_constraint(value, pltpu.VMEM) for value in (rows, gate_b, up_b, down_b)
    )
    return pl.pallas_call(
        expert_kernel,
        out_shape=pltpu.VMEM((count, depth), jnp.bfloat16),
        in_specs=[pl.BlockSpec(memory_space=pltpu.SMEM), vmem] + [hbm] * 3 + [vmem] * 3,
        out_specs=vmem,
        scratch_shapes=[
            pltpu.VMEM((depth, share), jnp.bfloat16),
            pltpu.VMEM((depth, share), jnp.bfloat16),
            pltpu.VMEM((share, depth), jnp.bfloat16),
            pltpu.VMEM((count, 2 * share), jnp.bfloat16),
            pltpu.SemaphoreType.DMA((6,)),
        ],
        compiler_params=pltpu.CompilerParams(vmem_limit_bytes=24 * MIB),
        cost_estimate=pl.CostEstimate(
            flops=2 * count * depth * share * 6,
            bytes_accessed=2 * (2 * count * depth + 6 * depth * share),
            transcendentals=count * share * 2,
        ),
        name="expert",
    )(core, rows, gate_a, up_a, down_a, gate_b, up_b, down_b)


def project_kernel(place_ref, rows_ref, *refs):
    *weights, out_ref = refs
    kinds = len(weights) // 2
    half, width = weights[0].shape[1:]
    ring = kinds - 1
    pair, turn, core = place_ref[0], place_ref[1], place_ref[2]
    near = rows_ref[:, pl.ds(pl.multiple_of(core * half, half), half)]
    far = rows_ref[:, pl.ds(pl.multiple_of((1 - core) * half, half), half)]
    for step in range(ring):
        total = None
        for rows, (own, before, after, first, second) in ((near, weights[:kinds]), (far, weights[kinds:])):
            if step == 2:
                both = jnp.concatenate([first[...], second[...]], axis=1)
            else:
                weight = {0: own, 1: before, 3: after}[step]
                both = jnp.concatenate([weight[0], weight[1]], axis=1)
            term = jnp.dot(rows, both, preferred_element_type=jnp.float32)
            total = term if total is None else total + term
        total = total.astype(out_ref.dtype)
        for which in range(2):
            owner = (pair + which) % 2 * ring + (turn + ring - step) % ring
            cols = pl.ds(pl.multiple_of(owner * width, width), width)
            out_ref[:, cols] = total[:, which * width : (which + 1) * width]


def run_project(place, rows, weights):
    count, depth = rows.shape
    width = 8 * weights[0].shape[2]
    vmem = pl.BlockSpec(memory_space=pltpu.VMEM)
    weights = [pltpu.with_memory_space_constraint(value, pltpu.VMEM) for value in weights]
    return pl.pallas_call(
        project_kernel,
        out_shape=pltpu.VMEM((count, width), jnp.bfloat16),
        in_specs=[pl.BlockSpec(memory_space=pltpu.SMEM)] + [vmem] * (1 + len(weights)),
        out_specs=vmem,
        compiler_params=pltpu.CompilerParams(vmem_limit_bytes=16 * MIB),
        cost_estimate=pl.CostEstimate(
            flops=2 * count * depth * width,
            bytes_accessed=2 * (count * depth + count * width + depth * width),
            transcendentals=0,
        ),
        name="project",
    )(place, rows, *weights)


def norm_kernel(terms_ref, residual_ref, gain_ref, out_ref, normed_ref, *, parts):
    width = terms_ref.shape[2]
    streams = []
    squares = None
    groups = terms_ref.shape[0] // parts
    outer = parts // 2
    for group in range(groups):
        cols = slice(group * width, (group + 1) * width)
        total = None
        for part in range(outer):
            for inner in range(2):
                term = terms_ref[(part * groups + group) * 2 + inner].astype(jnp.float32)
                total = term if total is None else total + term
        total = total.astype(jnp.bfloat16)
        out_ref[:, cols] = total
        stream = residual_ref[:, cols].astype(jnp.float32) + total.astype(jnp.float32)
        square = jnp.sum(stream * stream, axis=1, keepdims=True)
        squares = square if squares is None else squares + square
        streams.append(stream)
    scale = lax.rsqrt(squares / out_ref.shape[1] + 1e-06)
    for group, stream in enumerate(streams):
        cols = slice(group * width, (group + 1) * width)
        normed_ref[:, cols] = (stream * scale * gain_ref[:, cols]).astype(jnp.bfloat16)


def run_norm(terms, residual, gain, parts):
    vmem = pl.BlockSpec(memory_space=pltpu.VMEM)
    return pl.pallas_call(
        functools.partial(norm_kernel, parts=parts),
        out_shape=[jax.ShapeDtypeStruct(residual.shape, jnp.bfloat16)] * 2,
        in_specs=[vmem] * 3,
        out_specs=[vmem] * 2,
        compiler_params=pltpu.CompilerParams(vmem_limit_bytes=16 * MIB),
        cost_estimate=pl.CostEstimate(
            flops=2 * terms.size, bytes_accessed=2 * terms.size, transcendentals=0
        ),
        name="norm",
    )(terms, residual, gain.reshape(1, -1))


def place_kernel(placing_ref, own_ref, other_ref, out_ref):
    count = placing_ref.shape[0]
    step = count // 4
    rows = jnp.concatenate([own_ref[...], other_ref[...]], axis=0)
    for start in range(0, count, step):
        value = jnp.dot(placing_ref[start : start + step, :], rows, preferred_element_type=jnp.float32)
        value = value.astype(out_ref.dtype)
        for copy in range(2):
            out_ref[copy * count + start : copy * count + start + step, :] = value


def run_place(placing, own, other):
    vmem = pl.BlockSpec(memory_space=pltpu.VMEM)
    count, depth = placing.shape[0], own.shape[1]
    return pl.pallas_call(
        place_kernel,
        out_shape=pltpu.VMEM((2 * count, depth), jnp.bfloat16),
        in_specs=[vmem] * 3,
        out_specs=vmem,
        compiler_params=pltpu.CompilerParams(vmem_limit_bytes=16 * MIB),
        cost_estimate=pl.CostEstimate(
            flops=2 * placing.size * depth, bytes_accessed=4 * count * depth, transcendentals=0
        ),
        name="place",
    )(placing, own, other)


def swap(value):
    return lax.ppermute(value, "core", SWAP)


def places(expert_ids, core, expert_total):
    row_count = expert_ids.shape[0]
    pair_ids = expert_ids.reshape(-1)
    member = (pair_ids[:, None] == jnp.arange(expert_total, dtype=jnp.int32)[None, :]).astype(
        jnp.int32
    )
    ranking = jnp.sum((jnp.cumsum(member, 0) - 1) * member, 1)
    here = (pair_ids % 2) == core
    slot = (pair_ids // 2) * (2 * SLOTS) + ranking
    slot = jnp.where(here, slot, -1)
    return slot.reshape(row_count, TOP)


def on_device(
    queries,
    kv_cache,
    kv_new,
    lengths,
    residual,
    norm_gain,
    expert_ids,
    route_probs,
    w_out,
    w_gate,
    w_up,
    w_down,
):
    row_count = queries.shape[0]
    core = lax.axis_index("core")
    core_index = core.astype(jnp.int32).reshape(1)
    ep_size = lax.axis_size(EP)
    plane = lax.axis_size(PLANE)
    chips = lax.axis_size(CHIPS)
    ring = lax.axis_size("z")
    parts = 2 * lax.axis_size("xh")
    depth = w_out.shape[0] // parts
    half = depth // 2

    pair = lax.axis_index("yl")
    quarter = lax.axis_index("xh") * 2
    given = lax.dynamic_slice_in_dim(w_out, (quarter + 1 - pair) * depth + core * half, half, axis=0)
    given, w_rest = lax.optimization_barrier((given, w_out))
    kept = lax.dynamic_slice_in_dim(w_rest, (quarter + pair) * depth + core * half, half, axis=0)
    taken = lax.ppermute(given, "yl", SWAP)
    sent = run_attend(queries, kv_cache, kv_new, lengths, parts, plane // parts)
    sent, taken, expert_ids, route_probs = lax.optimization_barrier((sent, taken, expert_ids, route_probs))
    own = jnp.stack([kept, taken])
    forth = [(at, (at + 1) % ring) for at in range(ring)]
    back = [(at, (at + ring - 1) % ring) for at in range(ring)]
    before = lax.ppermute(own, "z", forth)
    after = lax.ppermute(own, "z", back)
    expert_total = w_gate.shape[0] * ep_size
    slot_total = 2 * SLOTS * ep_size
    gates = route_probs / jnp.sum(route_probs, -1, keepdims=True)
    own_slots = places(expert_ids, core, expert_total)
    other_slots = places(swap(expert_ids), core, expert_total)
    other_slots = jnp.where(other_slots >= 0, other_slots + SLOTS, -1)
    slots = jnp.concatenate([own_slots, other_slots], 0)
    both_gates = jnp.concatenate([gates, swap(gates)], 0)
    chosen = slots[:, :, None] == jnp.arange(slot_total, dtype=jnp.int32)[None, None, :]
    placing = jnp.any(chosen, 1)
    mixing = jnp.sum(jnp.where(chosen, both_gates[:, :, None], 0.0), 1)
    placing = placing.astype(jnp.bfloat16).T
    mixing = jnp.concatenate([mixing, mixing], 1)
    mixing_high = mixing.astype(jnp.bfloat16)
    mixing_low = (mixing - mixing_high.astype(jnp.float32)).astype(jnp.bfloat16)
    mixing = jnp.concatenate([mixing_high, mixing_low], 0)

    passed, placing, mixing = lax.optimization_barrier((before[0], placing, mixing))
    weights = [own, before, after, lax.ppermute(passed, "z", forth), lax.ppermute(after[1], "z", back)]
    given = lax.optimization_barrier(weights[:4])
    weights += [swap(value) for value in given + weights[4:]]
    place = jnp.stack([pair, lax.axis_index("z"), core]).astype(jnp.int32)
    gathered = lax.all_to_all(sent, PLANE, split_axis=0, concat_axis=0, tiled=True)
    columns = run_project(place, gathered.reshape(plane * row_count, depth), weights)
    terms = lax.all_to_all(
        columns.reshape(plane, row_count, -1), PLANE, split_axis=0, concat_axis=0, tiled=True
    )
    attn_out, normed = run_norm(terms, residual, norm_gain, parts)

    other_normed = swap(normed)
    other_normed, w_gate, w_up, w_down = lax.optimization_barrier((other_normed, w_gate, w_up, w_down))
    gate_b, up_b, down_b = swap(w_gate), swap(w_up), swap(w_down)
    outgoing = run_place(placing, normed, other_normed)
    arrived = lax.all_to_all(
        outgoing.reshape(chips, 2 * SLOTS, -1), CHIPS, split_axis=0, concat_axis=0, tiled=True
    )
    partial_value = run_expert(
        core_index,
        arrived.reshape(chips * 2 * SLOTS, -1),
        w_gate,
        w_up,
        w_down,
        gate_b,
        up_b,
        down_b,
    )
    returned = lax.all_to_all(
        partial_value.reshape(chips, 2 * SLOTS, -1), CHIPS, split_axis=0, concat_axis=0, tiled=True
    )
    mixed = jnp.dot(
        mixing, returned.reshape(chips * 2 * SLOTS, -1), preferred_element_type=jnp.float32
    )
    mixed = mixed[: 2 * row_count] + mixed[2 * row_count :]
    moe_out = mixed[:row_count] + swap(mixed[row_count:].astype(jnp.bfloat16)).astype(jnp.float32)
    return (attn_out, moe_out.astype(jnp.bfloat16))


def solution(mesh):
    fine = Mesh(mesh.devices.reshape(2, 2, 2, 2, 2, 4), ALL)
    return jax.shard_map(
        on_device,
        mesh=fine,
        in_specs=(
            P(ALL, None),
            P(ALL, None, None, None),
            P(ALL, None, None),
            P(ALL),
            P(ALL, None),
            P(),
            P(ALL, None),
            P(ALL, None),
            P(None, EP),
            P(EP, None, DP),
            P(EP, None, DP),
            P(EP, DP, None),
        ),
        out_specs=(P(ALL, None), P(ALL, None)),
        check_vma=False,
    )
```

```python
import functools
import math

import jax
import jax.numpy as jnp
from jax import lax
from jax.experimental import pallas as pl
from jax.experimental.pallas import tpu as pltpu
from jax.sharding import Mesh, PartitionSpec as P

HEADS = 64
KVH = 4
HD = 128
TOP = 8
SLOTS = 4

DP = ("xh", "core")
EP = ("xl", "yh", "yl", "z")
PLANE = ("xh", "xl", "yh", "yl")
CHIPS = ("yh", "yl", "xl", "xh", "z")
ALL = DP + EP
SWAP = ((0, 1), (1, 0))
MIB = 1 << 20
RUN = 8 * SLOTS
BLOCK = 128
WIDE = 1024


def attend_kernel(
    lengths_hbm, queries_hbm, cache_hbm, fresh_hbm, out_ref, lengths_ref, queries_ref, cache, fresh_ref, heads, sems, *, parts, copies
):
    rows = queries_ref.shape[0]
    batches = sems.shape[0] - 3
    batch = rows // batches
    span = cache.shape[2]
    others = [
        pltpu.make_async_copy(queries_hbm, queries_ref, sems.at[batches]),
        pltpu.make_async_copy(fresh_hbm, fresh_ref, sems.at[batches + 1]),
        pltpu.make_async_copy(lengths_hbm, lengths_ref, sems.at[batches + 2]),
    ]
    for other in others:
        other.start()
    moves = []
    for number in range(batches):
        at = pl.ds(number * batch, batch)
        moves.append(pltpu.make_async_copy(cache_hbm.at[at], cache.at[at], sems.at[number]))
        moves[-1].start()
    groups = HEADS // KVH
    scaling = 1.0 / math.sqrt(HD)
    for other in others:
        other.wait()
    for head in range(HEADS):
        query = queries_ref[:, head * HD : (head + 1) * HD].astype(jnp.float32)
        heads[pl.ds(head, rows, stride=HEADS), :] = query
    position = lax.broadcasted_iota(jnp.int32, (HEADS, span), 1)
    for number, move in enumerate(moves):
        move.wait()
        those = range(number * batch, (number + 1) * batch)
        at = slice(number * batch * HEADS, (number + 1) * batch * HEADS)
        query = heads[at, :]
        rounded = query.astype(jnp.bfloat16)
        blocks = [
            (row, kv, slice(kv * HD, (kv + 1) * HD), slice(place * groups, (place + 1) * groups))
            for place, (row, kv) in enumerate((row, kv) for row in those for kv in range(KVH))
        ]
        scores = jnp.concatenate(
            [
                lax.dot_general(
                    rounded[own], cache[row, 0, :, cols], (((1,), (1,)), ((), ())), preferred_element_type=jnp.float32
                )
                for row, kv, cols, own in blocks
            ],
            axis=0,
        )
        keys = [
            jnp.broadcast_to(fresh_ref[row, 0:1, cols].astype(jnp.float32), (groups, HD)) for row, kv, cols, own in blocks
        ]
        fresh = jnp.sum(query * jnp.concatenate(keys, axis=0), axis=1, keepdims=True) * scaling
        live = jnp.concatenate([position < lengths_ref[row] for row in those], axis=0)
        scores = jnp.where(live, scores * scaling, -1e30)
        highest = jnp.maximum(jnp.max(scores, axis=1, keepdims=True), fresh)
        scores = jnp.exp(scores - highest)
        fresh = jnp.exp(fresh - highest)
        denominator = jnp.sum(scores, axis=1, keepdims=True) + fresh
        weights = (scores / denominator).astype(jnp.bfloat16)
        fresh = (fresh / denominator).astype(jnp.bfloat16).astype(jnp.float32)
        mixed = [
            jnp.dot(weights[own], cache[row, 1, :, cols], preferred_element_type=jnp.float32)
            + fresh[own] * fresh_ref[row, 1:2, cols].astype(jnp.float32)
            for row, kv, cols, own in blocks
        ]
        heads[at, :] = jnp.concatenate(mixed, axis=0)
    share = HEADS // parts
    for head in range(HEADS):
        value = heads[pl.ds(head, rows, stride=HEADS), :].astype(jnp.bfloat16)
        cols = slice(head % share * HD, (head % share + 1) * HD)
        outer, inner = divmod(head // share, 2)
        for copy in range(copies):
            out_ref[(outer * copies + copy) * 2 + inner, :, cols] = value

def run_attend(queries, kv_cache, kv_new, lengths, parts, copies):
    rows = queries.shape[0]
    hbm = pl.BlockSpec(memory_space=pltpu.HBM)
    operands = [pltpu.with_memory_space_constraint(value, pltpu.HBM) for value in (lengths, queries, kv_cache, kv_new)]
    return pl.pallas_call(
        functools.partial(attend_kernel, parts=parts, copies=copies),
        out_shape=pltpu.HBM((copies * parts, rows, HEADS * HD // parts), jnp.bfloat16),
        in_specs=[hbm] * 4,
        out_specs=pl.BlockSpec(memory_space=pltpu.VMEM),
        scratch_shapes=[
            pltpu.SMEM(lengths.shape, jnp.int32),
            pltpu.VMEM(queries.shape, jnp.bfloat16),
            pltpu.VMEM(kv_cache.shape, jnp.bfloat16),
            pltpu.VMEM(kv_new.shape, jnp.bfloat16),
            pltpu.VMEM((rows * HEADS, HD), jnp.float32),
            pltpu.SemaphoreType.DMA((7,)),
        ],
        compiler_params=pltpu.CompilerParams(vmem_limit_bytes=24 * MIB),
        cost_estimate=pl.CostEstimate(
            flops=4 * kv_cache.size // 2 * HEADS // KVH,
            bytes_accessed=2 * (kv_cache.size + 5 * queries.size),
            transcendentals=rows * HEADS * kv_cache.shape[2],
        ),
        name="attend",
    )(*operands)


def expert_kernel(
    core_ref, rows, gate_a, up_a, down_a, gate_b, up_b, down_b, out, gate, up, down, hidden, sems
):
    mine = core_ref[0]
    depth = rows.shape[1]
    share = gate.shape[1]
    moves = []
    for source, target in ((gate_a, gate), (up_a, up), (down_a, down)):
        size = target.shape[0] // 2
        for half in range(2):
            at = pl.ds(half * size, size)
            moves.append(pltpu.make_async_copy(source.at[mine, at], target.at[at], sems.at[len(moves)]))
            moves[-1].start()

    def step(gate_of, up_of, base):
        @pl.when(mine >= 0)
        def _():
            for start in range(0, share, BLOCK):
                cols = slice(start, start + BLOCK)
                both = jnp.concatenate([gate_of(cols), up_of(cols)], axis=1)
                acts = jnp.dot(rows[...], both, preferred_element_type=jnp.float32)
                gate_act = acts[:, :BLOCK]
                value = gate_act / (1.0 + jnp.exp(-gate_act)) * acts[:, BLOCK:]
                hidden[:, base + start : base + start + BLOCK] = value.astype(jnp.bfloat16)

    step(lambda cols: gate_b[mine, :, cols], lambda cols: up_b[mine, :, cols], 0)
    for move in moves[:4]:
        move.wait()
    step(lambda cols: gate[:, cols], lambda cols: up[:, cols], share)
    for move in moves[4:]:
        move.wait()

    @pl.when(mine >= 0)
    def _():
        for start in range(0, depth, WIDE):
            cols = slice(start, start + WIDE)
            both = jnp.concatenate([down_b[mine, :, cols], down[:, cols]], axis=0)
            out[:, cols] = jnp.dot(hidden[...], both, preferred_element_type=jnp.float32).astype(out.dtype)


def run_expert(core, rows, gate_a, up_a, down_a, gate_b, up_b, down_b):
    count, depth = rows.shape
    share = gate_a.shape[2]
    hbm = pl.BlockSpec(memory_space=pl.ANY)
    vmem = pl.BlockSpec(memory_space=pltpu.VMEM)
    rows, gate_b, up_b, down_b = (
        pltpu.with_memory_space_constraint(value, pltpu.VMEM) for value in (rows, gate_b, up_b, down_b)
    )
    return pl.pallas_call(
        expert_kernel,
        out_shape=pltpu.VMEM((count, depth), jnp.bfloat16),
        in_specs=[pl.BlockSpec(memory_space=pltpu.SMEM), vmem] + [hbm] * 3 + [vmem] * 3,
        out_specs=vmem,
        scratch_shapes=[
            pltpu.VMEM((depth, share), jnp.bfloat16),
            pltpu.VMEM((depth, share), jnp.bfloat16),
            pltpu.VMEM((share, depth), jnp.bfloat16),
            pltpu.VMEM((count, 2 * share), jnp.bfloat16),
            pltpu.SemaphoreType.DMA((6,)),
        ],
        compiler_params=pltpu.CompilerParams(vmem_limit_bytes=24 * MIB),
        cost_estimate=pl.CostEstimate(
            flops=2 * count * depth * share * 6,
            bytes_accessed=2 * (2 * count * depth + 6 * depth * share),
            transcendentals=count * share * 2,
        ),
        name="expert",
    )(core, rows, gate_a, up_a, down_a, gate_b, up_b, down_b)


def project_kernel(place_ref, rows_ref, *refs):
    *weights, out_ref = refs
    kinds = len(weights) // 2
    half, width = weights[0].shape[1:]
    ring = kinds - 1
    pair, turn, core = place_ref[0], place_ref[1], place_ref[2]
    near = rows_ref[:, pl.ds(pl.multiple_of(core * half, half), half)]
    far = rows_ref[:, pl.ds(pl.multiple_of((1 - core) * half, half), half)]
    for step in range(ring):
        total = None
        for rows, (own, before, after, first, second) in ((near, weights[:kinds]), (far, weights[kinds:])):
            if step == 2:
                both = jnp.concatenate([first[...], second[...]], axis=1)
            else:
                weight = {0: own, 1: before, 3: after}[step]
                both = jnp.concatenate([weight[0], weight[1]], axis=1)
            term = jnp.dot(rows, both, preferred_element_type=jnp.float32)
            total = term if total is None else total + term
        total = total.astype(out_ref.dtype)
        for which in range(2):
            owner = (pair + which) % 2 * ring + (turn + ring - step) % ring
            cols = pl.ds(pl.multiple_of(owner * width, width), width)
            out_ref[:, cols] = total[:, which * width : (which + 1) * width]


def run_project(place, rows, weights):
    count, depth = rows.shape
    width = 8 * weights[0].shape[2]
    vmem = pl.BlockSpec(memory_space=pltpu.VMEM)
    weights = [pltpu.with_memory_space_constraint(value, pltpu.VMEM) for value in weights]
    return pl.pallas_call(
        project_kernel,
        out_shape=pltpu.VMEM((count, width), jnp.bfloat16),
        in_specs=[pl.BlockSpec(memory_space=pltpu.SMEM)] + [vmem] * (1 + len(weights)),
        out_specs=vmem,
        compiler_params=pltpu.CompilerParams(vmem_limit_bytes=16 * MIB),
        cost_estimate=pl.CostEstimate(
            flops=2 * count * depth * width,
            bytes_accessed=2 * (count * depth + count * width + depth * width),
            transcendentals=0,
        ),
        name="project",
    )(place, rows, *weights)


def norm_kernel(terms_ref, residual_ref, gain_ref, out_ref, normed_ref, *, parts):
    width = terms_ref.shape[2]
    streams = []
    squares = None
    groups = terms_ref.shape[0] // parts
    outer = parts // 2
    for group in range(groups):
        cols = slice(group * width, (group + 1) * width)
        total = None
        for part in range(outer):
            for inner in range(2):
                term = terms_ref[(part * groups + group) * 2 + inner].astype(jnp.float32)
                total = term if total is None else total + term
        total = total.astype(jnp.bfloat16)
        out_ref[:, cols] = total
        stream = residual_ref[:, cols].astype(jnp.float32) + total.astype(jnp.float32)
        square = jnp.sum(stream * stream, axis=1, keepdims=True)
        squares = square if squares is None else squares + square
        streams.append(stream)
    scale = lax.rsqrt(squares / out_ref.shape[1] + 1e-06)
    for group, stream in enumerate(streams):
        cols = slice(group * width, (group + 1) * width)
        normed_ref[:, cols] = (stream * scale * gain_ref[:, cols]).astype(jnp.bfloat16)


def run_norm(terms, residual, gain, parts):
    vmem = pl.BlockSpec(memory_space=pltpu.VMEM)
    return pl.pallas_call(
        functools.partial(norm_kernel, parts=parts),
        out_shape=[jax.ShapeDtypeStruct(residual.shape, jnp.bfloat16)] * 2,
        in_specs=[vmem] * 3,
        out_specs=[vmem] * 2,
        compiler_params=pltpu.CompilerParams(vmem_limit_bytes=16 * MIB),
        cost_estimate=pl.CostEstimate(
            flops=2 * terms.size, bytes_accessed=2 * terms.size, transcendentals=0
        ),
        name="norm",
    )(terms, residual, gain.reshape(1, -1))


def place_kernel(placing_ref, own_ref, other_ref, out_ref):
    count = placing_ref.shape[0]
    step = count // 4
    rows = jnp.concatenate([own_ref[...], other_ref[...]], axis=0)
    for start in range(0, count, step):
        value = jnp.dot(placing_ref[start : start + step, :], rows, preferred_element_type=jnp.float32)
        value = value.astype(out_ref.dtype)
        for part in range(0, step, RUN):
            for copy in range(2):
                at = 2 * (start + part) + copy * RUN
                out_ref[at : at + RUN, :] = value[part : part + RUN, :]


def run_place(placing, own, other):
    vmem = pl.BlockSpec(memory_space=pltpu.VMEM)
    count, depth = placing.shape[0], own.shape[1]
    return pl.pallas_call(
        place_kernel,
        out_shape=pltpu.VMEM((2 * count, depth), jnp.bfloat16),
        in_specs=[vmem] * 3,
        out_specs=vmem,
        compiler_params=pltpu.CompilerParams(vmem_limit_bytes=16 * MIB),
        cost_estimate=pl.CostEstimate(
            flops=2 * placing.size * depth, bytes_accessed=4 * count * depth, transcendentals=0
        ),
        name="place",
    )(placing, own, other)


def swap(value):
    return lax.ppermute(value, "core", SWAP)


def places(expert_ids, core, expert_total):
    row_count = expert_ids.shape[0]
    pair_ids = expert_ids.reshape(-1)
    member = (pair_ids[:, None] == jnp.arange(expert_total, dtype=jnp.int32)[None, :]).astype(
        jnp.int32
    )
    ranking = jnp.sum((jnp.cumsum(member, 0) - 1) * member, 1)
    here = (pair_ids % 2) == core
    chip = pair_ids // 2
    chip = (chip // 4 % 4 * 2 + chip // 16) * 4 + chip % 4
    slot = chip * (2 * SLOTS) + ranking
    slot = jnp.where(here, slot, -1)
    return slot.reshape(row_count, TOP)


def on_device(
    queries,
    kv_cache,
    kv_new,
    lengths,
    residual,
    norm_gain,
    expert_ids,
    route_probs,
    w_out,
    w_gate,
    w_up,
    w_down,
):
    row_count = queries.shape[0]
    core = lax.axis_index("core")
    core_index = core.astype(jnp.int32).reshape(1)
    ep_size = lax.axis_size(EP)
    plane = lax.axis_size(PLANE)
    chips = lax.axis_size(CHIPS)
    ring = lax.axis_size("z")
    parts = 2 * lax.axis_size("xh")
    depth = w_out.shape[0] // parts
    half = depth // 2

    pair = lax.axis_index("yl")
    quarter = lax.axis_index("xh") * 2
    given = lax.dynamic_slice_in_dim(w_out, (quarter + 1 - pair) * depth + core * half, half, axis=0)
    given, w_rest = lax.optimization_barrier((given, w_out))
    kept = lax.dynamic_slice_in_dim(w_rest, (quarter + pair) * depth + core * half, half, axis=0)
    taken = lax.ppermute(given, "yl", SWAP)
    sent = run_attend(queries, kv_cache, kv_new, lengths, parts, plane // parts)
    sent, taken, expert_ids, route_probs = lax.optimization_barrier((sent, taken, expert_ids, route_probs))
    own = jnp.stack([kept, taken])
    forth = [(at, (at + 1) % ring) for at in range(ring)]
    back = [(at, (at + ring - 1) % ring) for at in range(ring)]
    before = lax.ppermute(own, "z", forth)
    after = lax.ppermute(own, "z", back)
    expert_total = w_gate.shape[0] * ep_size
    slot_total = 2 * SLOTS * ep_size
    gates = route_probs / jnp.sum(route_probs, -1, keepdims=True)
    own_slots = places(expert_ids, core, expert_total)
    other_slots = places(swap(expert_ids), core, expert_total)
    other_slots = jnp.where(other_slots >= 0, other_slots + SLOTS, -1)
    slots = jnp.concatenate([own_slots, other_slots], 0)
    both_gates = jnp.concatenate([gates, swap(gates)], 0)
    chosen = slots[:, :, None] == jnp.arange(slot_total, dtype=jnp.int32)[None, None, :]
    placing = jnp.any(chosen, 1)
    mixing = jnp.sum(jnp.where(chosen, both_gates[:, :, None], 0.0), 1)
    placing = placing.astype(jnp.bfloat16).T
    mixing = mixing.reshape(2 * row_count, -1, 1, RUN)
    mixing = jnp.concatenate([mixing, mixing], 2).reshape(2 * row_count, 2 * slot_total)
    mixing_high = mixing.astype(jnp.bfloat16)
    mixing_low = (mixing - mixing_high.astype(jnp.float32)).astype(jnp.bfloat16)
    mixing = jnp.concatenate([mixing_high, mixing_low], 0)

    passed, placing, mixing = lax.optimization_barrier((before[0], placing, mixing))
    weights = [own, before, after, lax.ppermute(passed, "z", forth), lax.ppermute(after[1], "z", back)]
    first = lax.optimization_barrier(weights[:3])
    weights += [swap(value) for value in first + weights[3:]]
    place = jnp.stack([pair, lax.axis_index("z"), core]).astype(jnp.int32)
    gathered = lax.all_to_all(sent, PLANE, split_axis=0, concat_axis=0, tiled=True)
    columns = run_project(place, gathered.reshape(plane * row_count, depth), weights)
    terms = lax.all_to_all(
        columns.reshape(plane, row_count, -1), PLANE, split_axis=0, concat_axis=0, tiled=True
    )
    attn_out, normed = run_norm(terms, residual, norm_gain, parts)

    other_normed = swap(normed)
    other_normed, w_gate, w_up, w_down = lax.optimization_barrier((other_normed, w_gate, w_up, w_down))
    gate_b, up_b, down_b = swap(w_gate), swap(w_up), swap(w_down)
    outgoing = run_place(placing, normed, other_normed)
    arrived = lax.all_to_all(
        outgoing.reshape(chips, 2 * SLOTS, -1), CHIPS, split_axis=0, concat_axis=0, tiled=True
    )
    partial_value = run_expert(
        core_index,
        arrived.reshape(chips * 2 * SLOTS, -1),
        w_gate,
        w_up,
        w_down,
        gate_b,
        up_b,
        down_b,
    )
    returned = lax.all_to_all(
        partial_value.reshape(chips, 2 * SLOTS, -1), CHIPS, split_axis=0, concat_axis=0, tiled=True
    )
    mixed = jnp.dot(
        mixing, returned.reshape(chips * 2 * SLOTS, -1), preferred_element_type=jnp.float32
    )
    mixed = mixed[: 2 * row_count] + mixed[2 * row_count :]
    moe_out = mixed[:row_count] + swap(mixed[row_count:].astype(jnp.bfloat16)).astype(jnp.float32)
    return (attn_out, moe_out.astype(jnp.bfloat16))


def solution(mesh):
    fine = Mesh(mesh.devices.reshape(2, 2, 2, 2, 2, 4), ALL)
    return jax.shard_map(
        on_device,
        mesh=fine,
        in_specs=(
            P(ALL, None),
            P(ALL, None, None, None),
            P(ALL, None, None),
            P(ALL),
            P(ALL, None),
            P(),
            P(ALL, None),
            P(ALL, None),
            P(None, EP),
            P(EP, None, DP),
            P(EP, None, DP),
            P(EP, DP, None),
        ),
        out_specs=(P(ALL, None), P(ALL, None)),
        check_vma=False,
    )
```

```python
import functools
import math

import jax
import jax.numpy as jnp
from jax import lax
from jax.experimental import pallas as pl
from jax.experimental.pallas import tpu as pltpu
from jax.sharding import Mesh, PartitionSpec as P

HEADS = 64
KVH = 4
HD = 128
TOP = 8
SLOTS = 4

DP = ("xh", "core")
EP = ("xl", "yh", "yl", "z")
PLANE = ("xh", "xl", "yh", "yl")
CHIPS = ("yh", "yl", "xl", "xh", "z")
ALL = DP + EP
SWAP = ((0, 1), (1, 0))
MIB = 1 << 20
RUN = 8 * SLOTS
BLOCK = 128
WIDE = 1024


def attend_kernel(
    lengths_hbm, queries_hbm, cache_hbm, fresh_hbm, out_ref, lengths_ref, queries_ref, cache, fresh_ref, heads, sems, *, parts, copies
):
    rows = queries_ref.shape[0]
    batches = sems.shape[0] - 3
    batch = rows // batches
    span = cache.shape[2]
    others = [
        pltpu.make_async_copy(queries_hbm, queries_ref, sems.at[batches]),
        pltpu.make_async_copy(fresh_hbm, fresh_ref, sems.at[batches + 1]),
        pltpu.make_async_copy(lengths_hbm, lengths_ref, sems.at[batches + 2]),
    ]
    for other in others:
        other.start()
    moves = []
    for number in range(batches):
        at = pl.ds(number * batch, batch)
        moves.append(pltpu.make_async_copy(cache_hbm.at[at], cache.at[at], sems.at[number]))
        moves[-1].start()
    groups = HEADS // KVH
    scaling = 1.0 / math.sqrt(HD)
    for other in others:
        other.wait()
    for head in range(HEADS):
        query = queries_ref[:, head * HD : (head + 1) * HD].astype(jnp.float32)
        heads[pl.ds(head, rows, stride=HEADS), :] = query
    position = lax.broadcasted_iota(jnp.int32, (HEADS, span), 1)
    for number, move in enumerate(moves):
        move.wait()
        those = range(number * batch, (number + 1) * batch)
        at = slice(number * batch * HEADS, (number + 1) * batch * HEADS)
        query = heads[at, :]
        rounded = query.astype(jnp.bfloat16)
        blocks = [
            (row, kv, slice(kv * HD, (kv + 1) * HD), slice(place * groups, (place + 1) * groups))
            for place, (row, kv) in enumerate((row, kv) for row in those for kv in range(KVH))
        ]
        scores = jnp.concatenate(
            [
                lax.dot_general(
                    rounded[own], cache[row, 0, :, cols], (((1,), (1,)), ((), ())), preferred_element_type=jnp.float32
                )
                for row, kv, cols, own in blocks
            ],
            axis=0,
        )
        keys = [
            jnp.broadcast_to(fresh_ref[row, 0:1, cols], (groups, HD)) for row, kv, cols, own in blocks
        ]
        fresh = jnp.sum(query * jnp.concatenate(keys, axis=0), axis=1, keepdims=True) * scaling
        live = jnp.concatenate([position < lengths_ref[row] for row in those], axis=0)
        scores = jnp.where(live, scores * scaling, -1e30)
        highest = jnp.maximum(jnp.max(scores, axis=1, keepdims=True), fresh)
        scores = jnp.exp(scores - highest)
        fresh = jnp.exp(fresh - highest)
        denominator = jnp.sum(scores, axis=1, keepdims=True) + fresh
        weights = (scores / denominator).astype(jnp.bfloat16)
        fresh = (fresh / denominator).astype(jnp.bfloat16).astype(jnp.float32)
        mixed = [
            jnp.dot(weights[own], cache[row, 1, :, cols], preferred_element_type=jnp.float32)
            + fresh[own] * fresh_ref[row, 1:2, cols]
            for row, kv, cols, own in blocks
        ]
        heads[at, :] = jnp.concatenate(mixed, axis=0)
    share = HEADS // parts
    for head in range(HEADS):
        value = heads[pl.ds(head, rows, stride=HEADS), :].astype(jnp.bfloat16)
        cols = slice(head % share * HD, (head % share + 1) * HD)
        outer, inner = divmod(head // share, 2)
        for copy in range(copies):
            out_ref[(outer * copies + copy) * 2 + inner, :, cols] = value

def run_attend(queries, kv_cache, kv_new, lengths, parts, copies):
    rows = queries.shape[0]
    hbm = pl.BlockSpec(memory_space=pltpu.HBM)
    operands = [pltpu.with_memory_space_constraint(value, pltpu.HBM) for value in (lengths, queries, kv_cache, kv_new.astype(jnp.float32))]
    return pl.pallas_call(
        functools.partial(attend_kernel, parts=parts, copies=copies),
        out_shape=pltpu.HBM((copies * parts, rows, HEADS * HD // parts), jnp.bfloat16),
        in_specs=[hbm] * 4,
        out_specs=pl.BlockSpec(memory_space=pltpu.VMEM),
        scratch_shapes=[
            pltpu.SMEM(lengths.shape, jnp.int32),
            pltpu.VMEM(queries.shape, jnp.bfloat16),
            pltpu.VMEM(kv_cache.shape, jnp.bfloat16),
            pltpu.VMEM(kv_new.shape, jnp.float32),
            pltpu.VMEM((rows * HEADS, HD), jnp.float32),
            pltpu.SemaphoreType.DMA((7,)),
        ],
        compiler_params=pltpu.CompilerParams(vmem_limit_bytes=24 * MIB),
        cost_estimate=pl.CostEstimate(
            flops=4 * kv_cache.size // 2 * HEADS // KVH,
            bytes_accessed=2 * (kv_cache.size + 5 * queries.size),
            transcendentals=rows * HEADS * kv_cache.shape[2],
        ),
        name="attend",
    )(*operands)


def expert_kernel(
    core_ref, rows, gate_a, up_a, down_a, gate_b, up_b, down_b, out, gate, up, down, hidden, sems
):
    mine = core_ref[0]
    depth = rows.shape[1]
    share = gate.shape[1]
    moves = []
    for source, target in ((gate_a, gate), (up_a, up), (down_a, down)):
        size = target.shape[0] // 2
        for half in range(2):
            at = pl.ds(half * size, size)
            moves.append(pltpu.make_async_copy(source.at[mine, at], target.at[at], sems.at[len(moves)]))
            moves[-1].start()

    def step(gate_of, up_of, base):
        @pl.when(mine >= 0)
        def _():
            for start in range(0, share, BLOCK):
                cols = slice(start, start + BLOCK)
                both = jnp.concatenate([gate_of(cols), up_of(cols)], axis=1)
                acts = jnp.dot(rows[...], both, preferred_element_type=jnp.float32)
                gate_act = acts[:, :BLOCK]
                value = gate_act / (1.0 + jnp.exp(-gate_act)) * acts[:, BLOCK:]
                hidden[:, base + start : base + start + BLOCK] = value.astype(jnp.bfloat16)

    step(lambda cols: gate_b[mine, :, cols], lambda cols: up_b[mine, :, cols], 0)
    for move in moves[:4]:
        move.wait()
    step(lambda cols: gate[:, cols], lambda cols: up[:, cols], share)
    for move in moves[4:]:
        move.wait()

    @pl.when(mine >= 0)
    def _():
        for start in range(0, depth, WIDE):
            cols = slice(start, start + WIDE)
            both = jnp.concatenate([down_b[mine, :, cols], down[:, cols]], axis=0)
            out[:, cols] = jnp.dot(hidden[...], both, preferred_element_type=jnp.float32).astype(out.dtype)


def run_expert(core, rows, gate_a, up_a, down_a, gate_b, up_b, down_b):
    count, depth = rows.shape
    share = gate_a.shape[2]
    hbm = pl.BlockSpec(memory_space=pl.ANY)
    vmem = pl.BlockSpec(memory_space=pltpu.VMEM)
    rows, gate_b, up_b, down_b = (
        pltpu.with_memory_space_constraint(value, pltpu.VMEM) for value in (rows, gate_b, up_b, down_b)
    )
    return pl.pallas_call(
        expert_kernel,
        out_shape=pltpu.VMEM((count, depth), jnp.bfloat16),
        in_specs=[pl.BlockSpec(memory_space=pltpu.SMEM), vmem] + [hbm] * 3 + [vmem] * 3,
        out_specs=vmem,
        scratch_shapes=[
            pltpu.VMEM((depth, share), jnp.bfloat16),
            pltpu.VMEM((depth, share), jnp.bfloat16),
            pltpu.VMEM((share, depth), jnp.bfloat16),
            pltpu.VMEM((count, 2 * share), jnp.bfloat16),
            pltpu.SemaphoreType.DMA((6,)),
        ],
        compiler_params=pltpu.CompilerParams(vmem_limit_bytes=24 * MIB),
        cost_estimate=pl.CostEstimate(
            flops=2 * count * depth * share * 6,
            bytes_accessed=2 * (2 * count * depth + 6 * depth * share),
            transcendentals=count * share * 2,
        ),
        name="expert",
    )(core, rows, gate_a, up_a, down_a, gate_b, up_b, down_b)


def project_kernel(place_ref, rows_ref, *refs, other):
    *weights, out_ref = refs
    sums_ref = weights.pop() if other else None
    own, before, after, first, second = weights
    half, width = own.shape[1:]
    pairs = ((own, own), (before, before), (first, second), (after, after))
    ring = len(pairs)
    pair, turn, core = place_ref[0], place_ref[1], place_ref[2]
    side = 1 - core if other else core
    rows = rows_ref[:, pl.ds(pl.multiple_of(side * half, half), half)]
    for step, (left, right) in enumerate(pairs):
        if left is right:
            both = jnp.concatenate([left[0], right[1]], axis=1)
        else:
            both = jnp.concatenate([left[...], right[...]], axis=1)
        total = jnp.dot(rows, both, preferred_element_type=jnp.float32)
        cols = slice(2 * step * width, 2 * (step + 1) * width)
        if not other:
            out_ref[:, cols] = total
            continue
        total = (total + sums_ref[:, cols]).astype(out_ref.dtype)
        for which in range(2):
            owner = (pair + which) % 2 * ring + (turn + ring - step) % ring
            at = pl.ds(pl.multiple_of(owner * width, width), width)
            out_ref[:, at] = total[:, which * width : (which + 1) * width]


def run_project(place, rows, weights, sums=None):
    count, depth = rows.shape
    width = 8 * weights[0].shape[2]
    vmem = pl.BlockSpec(memory_space=pltpu.VMEM)
    other = sums is not None
    operands = [rows, *weights] + ([sums] if other else [])
    operands = [pltpu.with_memory_space_constraint(value, pltpu.VMEM) for value in operands]
    return pl.pallas_call(
        functools.partial(project_kernel, other=other),
        out_shape=pltpu.VMEM((count, width), jnp.bfloat16 if other else jnp.float32),
        in_specs=[pl.BlockSpec(memory_space=pltpu.SMEM)] + [vmem] * len(operands),
        out_specs=vmem,
        compiler_params=pltpu.CompilerParams(vmem_limit_bytes=16 * MIB),
        cost_estimate=pl.CostEstimate(
            flops=count * depth * width,
            bytes_accessed=count * depth + depth * width + 6 * count * width,
            transcendentals=0,
        ),
        name="project_other" if other else "project_own",
    )(place, *operands)


def norm_kernel(terms_ref, residual_ref, gain_ref, out_ref, normed_ref, *, parts):
    width = terms_ref.shape[2]
    streams = []
    squares = None
    groups = terms_ref.shape[0] // parts
    outer = parts // 2
    for group in range(groups):
        cols = slice(group * width, (group + 1) * width)
        total = None
        for part in range(outer):
            for inner in range(2):
                term = terms_ref[(part * groups + group) * 2 + inner].astype(jnp.float32)
                total = term if total is None else total + term
        total = total.astype(jnp.bfloat16)
        out_ref[:, cols] = total
        stream = residual_ref[:, cols].astype(jnp.float32) + total.astype(jnp.float32)
        square = jnp.sum(stream * stream, axis=1, keepdims=True)
        squares = square if squares is None else squares + square
        streams.append(stream)
    scale = lax.rsqrt(squares / out_ref.shape[1] + 1e-06)
    for group, stream in enumerate(streams):
        cols = slice(group * width, (group + 1) * width)
        normed_ref[:, cols] = (stream * scale * gain_ref[:, cols]).astype(jnp.bfloat16)


def run_norm(terms, residual, gain, parts):
    vmem = pl.BlockSpec(memory_space=pltpu.VMEM)
    return pl.pallas_call(
        functools.partial(norm_kernel, parts=parts),
        out_shape=[jax.ShapeDtypeStruct(residual.shape, jnp.bfloat16)] * 2,
        in_specs=[vmem] * 3,
        out_specs=[vmem] * 2,
        compiler_params=pltpu.CompilerParams(vmem_limit_bytes=16 * MIB),
        cost_estimate=pl.CostEstimate(
            flops=2 * terms.size, bytes_accessed=2 * terms.size, transcendentals=0
        ),
        name="norm",
    )(terms, residual, gain.reshape(1, -1))


def place_kernel(placing_ref, own_ref, other_ref, out_ref):
    count = placing_ref.shape[0]
    step = count // 4
    rows = jnp.concatenate([own_ref[...], other_ref[...]], axis=0)
    for start in range(0, count, step):
        value = jnp.dot(placing_ref[start : start + step, :], rows, preferred_element_type=jnp.float32)
        value = value.astype(out_ref.dtype)
        for part in range(0, step, RUN):
            for copy in range(2):
                at = 2 * (start + part) + copy * RUN
                out_ref[at : at + RUN, :] = value[part : part + RUN, :]


def run_place(placing, own, other):
    vmem = pl.BlockSpec(memory_space=pltpu.VMEM)
    count, depth = placing.shape[0], own.shape[1]
    return pl.pallas_call(
        place_kernel,
        out_shape=pltpu.VMEM((2 * count, depth), jnp.bfloat16),
        in_specs=[vmem] * 3,
        out_specs=vmem,
        compiler_params=pltpu.CompilerParams(vmem_limit_bytes=16 * MIB),
        cost_estimate=pl.CostEstimate(
            flops=2 * placing.size * depth, bytes_accessed=4 * count * depth, transcendentals=0
        ),
        name="place",
    )(placing, own, other)


def swap(value):
    return lax.ppermute(value, "core", SWAP)


def places(expert_ids, core, expert_total):
    row_count = expert_ids.shape[0]
    pair_ids = expert_ids.reshape(-1)
    member = (pair_ids[:, None] == jnp.arange(expert_total, dtype=jnp.int32)[None, :]).astype(
        jnp.int32
    )
    ranking = jnp.sum((jnp.cumsum(member, 0) - 1) * member, 1)
    here = (pair_ids % 2) == core
    chip = pair_ids // 2
    chip = (chip // 4 % 4 * 2 + chip // 16) * 4 + chip % 4
    slot = chip * (2 * SLOTS) + ranking
    slot = jnp.where(here, slot, -1)
    return slot.reshape(row_count, TOP)


def on_device(
    queries,
    kv_cache,
    kv_new,
    lengths,
    residual,
    norm_gain,
    expert_ids,
    route_probs,
    w_out,
    w_gate,
    w_up,
    w_down,
):
    row_count = queries.shape[0]
    core = lax.axis_index("core")
    core_index = core.astype(jnp.int32).reshape(1)
    ep_size = lax.axis_size(EP)
    plane = lax.axis_size(PLANE)
    chips = lax.axis_size(CHIPS)
    ring = lax.axis_size("z")
    parts = 2 * lax.axis_size("xh")
    depth = w_out.shape[0] // parts
    half = depth // 2

    pair = lax.axis_index("yl")
    quarter = lax.axis_index("xh") * 2
    given = lax.dynamic_slice_in_dim(w_out, (quarter + 1 - pair) * depth + core * half, half, axis=0)
    given, w_rest = lax.optimization_barrier((given, w_out))
    kept = lax.dynamic_slice_in_dim(w_rest, (quarter + pair) * depth + core * half, half, axis=0)
    taken = lax.ppermute(given, "yl", SWAP)
    sent = run_attend(queries, kv_cache, kv_new, lengths, parts, plane // parts)
    sent, taken, expert_ids, route_probs = lax.optimization_barrier((sent, taken, expert_ids, route_probs))
    own = jnp.stack([kept, taken])
    forth = [(at, (at + 1) % ring) for at in range(ring)]
    back = [(at, (at + ring - 1) % ring) for at in range(ring)]
    before = lax.ppermute(own, "z", forth)
    after = lax.ppermute(own, "z", back)
    expert_total = w_gate.shape[0] * ep_size
    slot_total = 2 * SLOTS * ep_size
    gates = route_probs / jnp.sum(route_probs, -1, keepdims=True)
    own_slots = places(expert_ids, core, expert_total)
    other_slots = places(swap(expert_ids), core, expert_total)
    other_slots = jnp.where(other_slots >= 0, other_slots + SLOTS, -1)
    slots = jnp.concatenate([own_slots, other_slots], 0)
    both_gates = jnp.concatenate([gates, swap(gates)], 0)
    chosen = slots[:, :, None] == jnp.arange(slot_total, dtype=jnp.int32)[None, None, :]
    placing = jnp.any(chosen, 1)
    mixing = jnp.sum(jnp.where(chosen, both_gates[:, :, None], 0.0), 1)
    placing = placing.astype(jnp.bfloat16).T
    mixing = mixing.reshape(2 * row_count, -1, 1, RUN)
    mixing = jnp.concatenate([mixing, mixing], 2).reshape(2 * row_count, 2 * slot_total)
    mixing_high = mixing.astype(jnp.bfloat16)
    mixing_low = (mixing - mixing_high.astype(jnp.float32)).astype(jnp.bfloat16)
    mixing = jnp.concatenate([mixing_high, mixing_low], 0)

    passed, placing, mixing = lax.optimization_barrier((before[0], placing, mixing))
    weights = [own, before, after, lax.ppermute(passed, "z", forth), lax.ppermute(after[1], "z", back)]
    first = lax.optimization_barrier(weights[:3])
    others = [swap(value) for value in first + weights[3:]]
    place = jnp.stack([pair, lax.axis_index("z"), core]).astype(jnp.int32)
    gathered = lax.all_to_all(sent, PLANE, split_axis=0, concat_axis=0, tiled=True)
    gathered = gathered.reshape(plane * row_count, depth)
    columns = run_project(place, gathered, others, run_project(place, gathered, weights))
    terms = lax.all_to_all(
        columns.reshape(plane, row_count, -1), PLANE, split_axis=0, concat_axis=0, tiled=True
    )
    attn_out, normed = run_norm(terms, residual, norm_gain, parts)

    other_normed = swap(normed)
    other_normed, w_gate, w_up, w_down = lax.optimization_barrier((other_normed, w_gate, w_up, w_down))
    gate_b, up_b, down_b = swap(w_gate), swap(w_up), swap(w_down)
    outgoing = run_place(placing, normed, other_normed)
    arrived = lax.all_to_all(
        outgoing.reshape(chips, 2 * SLOTS, -1), CHIPS, split_axis=0, concat_axis=0, tiled=True
    )
    partial_value = run_expert(
        core_index,
        arrived.reshape(chips * 2 * SLOTS, -1),
        w_gate,
        w_up,
        w_down,
        gate_b,
        up_b,
        down_b,
    )
    returned = lax.all_to_all(
        partial_value.reshape(chips, 2 * SLOTS, -1), CHIPS, split_axis=0, concat_axis=0, tiled=True
    )
    mixed = jnp.dot(
        mixing, returned.reshape(chips * 2 * SLOTS, -1), preferred_element_type=jnp.float32
    )
    mixed = mixed[: 2 * row_count] + mixed[2 * row_count :]
    moe_out = mixed[:row_count] + swap(mixed[row_count:].astype(jnp.bfloat16)).astype(jnp.float32)
    return (attn_out, moe_out.astype(jnp.bfloat16))


def solution(mesh):
    fine = Mesh(mesh.devices.reshape(2, 2, 2, 2, 2, 4), ALL)
    return jax.shard_map(
        on_device,
        mesh=fine,
        in_specs=(
            P(ALL, None),
            P(ALL, None, None, None),
            P(ALL, None, None),
            P(ALL),
            P(ALL, None),
            P(),
            P(ALL, None),
            P(ALL, None),
            P(None, EP),
            P(EP, None, DP),
            P(EP, None, DP),
            P(EP, DP, None),
        ),
        out_specs=(P(ALL, None), P(ALL, None)),
        check_vma=False,
    )
```
